32 devices in a mesh: groups: 2 (over y), src: 4 (over x, core), tgt: 4 (over z).
Axes of the slice: x: 2, y: 2, z: 4, core: 2. Of those that a mesh axis runs over, the one named last changes fastest.
Arguments:
- tokens: bfloat16 [8192, 1024], P(('groups', 'src', 'tgt')), parts along dimension 0, may hold values from -6 to 6
- sentence_ids: int32 [32, 256], P(('groups', 'src', 'tgt')), parts along dimension 0, may hold values from 0 to 31, never falling along the last dimension, each value on 1 to 32 neighbouring positions
- inner_weight: bfloat16 [4096, 1024], P(('src', 'tgt')), may hold values from -0.1875 to 0.1875
- outer_weight: bfloat16 [4096, 1024], P(('src', 'tgt')), may hold values from -0.09375 to 0.09375
- grid_rows: int32 [1024], P(('groups', 'src', 'tgt')), parts along dimension 0, may hold values from 0 to 511, as said below
- candidates: int32 [8, 16], P(('groups', 'src')), parts along dimension 0, may hold values from 0 to 63, as said below
- targets: bfloat16 [32768, 1024], P(('groups', 'tgt')), parts along dimension 0, may hold values from -6 to 6
Outputs:
- matched: bfloat16 [1024, 1024], P(('groups', 'src', 'tgt')), parts along dimension 0
- log_mass: float32 [1024], P(('groups', 'src', 'tgt')), parts along dimension 0
The draws below stay inside these ranges and needn't reach their ends.
There are 2 independent parts, one for each index of `groups`. The reference program is written for one: setup_inputs(seed, part) draws one part's arguments, and reference() takes and returns one part's arrays. A program takes and returns all parts, laid end to end along the dimension named above; an argument that names none is the same for every part. Nothing has to cross between parts.
Inputs may be any that keep to these rules, and one draw needn't show every extreme that they name: `grid_rows`: A permutation of the 512 source rows. The sentences of the device at index d along src+tgt take exactly 8 rows of every aligned run of 128 rows, rows d * 8 to d * 8 + 7 of that run. `candidates`: row b lists 16 distinct target blocks for the source rows b * 128 to b * 128 + 127. Block g lies in grid column g // 16. A row names at most 4 blocks of one column, and exactly 4 blocks of some column.
All inputs are finite; a program needn't handle non-finite values.
Results may differ from the reference program's by a relative error of at most 0.0082.
Values may be sent and summed in bfloat16 or wider, within the bound.
No kernel may reach another device: no remote copies, remote signals or barrier semaphores. Data moves between devices by JAX's collectives and lax.ppermute only.
A program may use at most 128 MiB of HBM per device.

```python
import math
import jax
import jax.numpy as jnp
import numpy as np
from jax import lax

D = 1024
FF = 4096
TOK_DEV = 256
SENT_DEV = 32
MAXLEN = 32
TBLK = 256
TB_COL = 16
K = 16
MOST = 4
PDEV = 16
SPB = 8
SBLK = 128
NSB = 4
NS = 512
TOKENS = 4096
NTB = 64
NT = 16384
N_SRC = 4
N_TGT = 4


def draw_grid_rows(key, part):
    subkeys = jax.random.split(key, PDEV)
    orders = jax.vmap(lambda subkey: jax.random.permutation(subkey, SENT_DEV))(subkeys).astype(jnp.int32)
    ranks = jnp.argsort(orders, axis=1, stable=True).astype(jnp.int32)
    device = jnp.arange(PDEV, dtype=jnp.int32)[:, None]
    rows = ranks // SPB * SBLK + device * SPB + ranks % SPB
    return rows.reshape(-1).astype(jnp.int32)


def draw_candidates(key, part):
    heavy_key, order_key, local_key, final_key = jax.random.split(jax.random.fold_in(key, 7), 4)
    heavy = jax.random.randint(heavy_key, (N_SRC,), 0, N_TGT)
    tickets = N_TGT * MOST
    orders = jax.vmap(lambda subkey: jax.random.permutation(subkey, tickets))(jax.random.split(order_key, N_SRC)).astype(jnp.int32)
    columns = orders // MOST
    light = (columns != heavy[:, None]).astype(jnp.int32)
    arrange = jnp.argsort(light, axis=1, stable=True)
    chosen = jnp.take_along_axis(columns, arrange, axis=1)[:, :K]
    same = chosen[:, :, None] == chosen[:, None, :]
    lower = jnp.arange(K)[None, :] < jnp.arange(K)[:, None]
    ranks = jnp.sum((same & lower[None, :, :]).astype(jnp.int32), axis=2)
    local_orders = jax.vmap(lambda subkey: jax.random.permutation(subkey, TB_COL))(jax.random.split(local_key, N_SRC * N_TGT)).astype(jnp.int32)
    local_orders = local_orders.reshape(N_SRC, N_TGT, TB_COL)
    source_index = jnp.arange(N_SRC, dtype=jnp.int32)[:, None]
    local = local_orders[source_index, chosen, ranks]
    blocks = chosen * TB_COL + local
    shuffle = jax.vmap(lambda subkey: jax.random.permutation(subkey, K))(jax.random.split(final_key, N_SRC)).astype(jnp.int32)
    return jnp.take_along_axis(blocks, shuffle, axis=1).astype(jnp.int32)


def level_of(stream_key, dims, pieces, smallest, largest):
    loudness = 1.0
    for position, blocks in pieces:
        draws = jax.random.uniform(jax.random.fold_in(jax.random.fold_in(stream_key, 6), position), (blocks,), jnp.float32, smallest / len(pieces), largest / len(pieces))
        loudness = loudness * jnp.repeat(jnp.exp(draws), dims[position] // blocks).reshape((-1,) + (1,) * (len(dims) - 1 - position))
    return loudness


def length_profile(count, total, limit, lean):
    loads = [(1 << 20) // math.isqrt(standing ** lean) + 1 for standing in range(2, count + 1)]
    rest, given = total - limit - (count - 1), [1] * (count - 1)
    while rest > 0:
        free = [i for i in range(count - 1) if given[i] < limit]
        whole, remaining = sum([loads[i] for i in free]), rest
        for i in free:
            extra = min(limit - given[i], max(1, remaining * loads[i] // whole), rest)
            given[i] = given[i] + extra
            rest = rest - extra
    return np.array([limit] + given)


def uneven(own_key, count, total, bound, slope):
    if count == 2:
        one = jax.random.randint(own_key, (), max(1, total - bound), min(bound, total - 1) + 1)
        return jnp.stack([one, total - one])
    tallies = jnp.asarray(length_profile(count, total, bound, slope), jnp.int32)
    twos = (count - 1) // 2
    donor, receiver = tallies[1:1 + 2 * twos:2], tallies[2:2 + 2 * twos:2]
    margin = jnp.minimum(donor - 1, bound - receiver)
    shifted = jax.random.randint(jax.random.fold_in(own_key, 1), (twos,), 0, 1 << 20) % (margin + 1)
    tallies = tallies.at[1:1 + 2 * twos:2].set(donor - shifted).at[2:2 + 2 * twos:2].set(receiver + shifted)
    return tallies[jax.random.permutation(jax.random.fold_in(own_key, 2), count)]


def normal_values(stream_key, shape, deviation, limit, shards=(), kind=jnp.bfloat16):
    result = deviation * jax.random.normal(stream_key, shape, jnp.float32)
    if shards:
        result = result * level_of(stream_key, shape, shards, -0.22, 0.18)
    return jnp.clip(result, -limit, limit).astype(kind)


def setup_inputs(seed: int = 0, part: int = 0) -> dict:
    key_list = jax.random.split(jax.random.key(seed), 8)
    part_keys = jax.random.split(jax.random.fold_in(key_list[7], part), 8)
    tokens = normal_values(part_keys[0], (TOKENS, D), 1.0, 6.0, ((0, 16),))
    sentence_ids = jax.vmap(lambda own: jnp.searchsorted(jnp.cumsum(uneven(own, SENT_DEV, TOK_DEV, MAXLEN, 2)), jnp.arange(TOK_DEV), side="right"))(jax.random.split(part_keys[1], PDEV)).reshape((PDEV, TOK_DEV)).astype(jnp.int32)
    inner_weight = normal_values(key_list[2], (FF, D), D ** -0.5, 0.1875, ((0, 16),))
    outer_weight = normal_values(key_list[3], (FF, D), FF ** -0.5, 0.09375, ((0, 16),))
    grid_rows = draw_grid_rows(jax.random.fold_in(jax.random.fold_in(key_list[7], part), 71), part)
    candidates = draw_candidates(jax.random.fold_in(jax.random.fold_in(key_list[7], part), 71), part)
    targets = normal_values(part_keys[6], (NT, D), 1.0, 6.0, ((0, 4),))
    return dict(tokens=tokens, sentence_ids=sentence_ids, inner_weight=inner_weight, outer_weight=outer_weight, grid_rows=grid_rows, candidates=candidates, targets=targets)


SCORE_SCALE = 32.0

def unit_rows(values):
    floats = values.astype(jnp.float32)
    square = lax.optimization_barrier(jnp.mean(floats * floats, axis=-1, keepdims=True))
    return (floats * lax.rsqrt(square + 1e-06) * (1.0 / math.sqrt(values.shape[-1]))).astype(jnp.bfloat16)

def inner_units(rows, inner):
    product = lax.dot_general(rows, inner, (((1,), (1,)), ((), ())), preferred_element_type=jnp.float32)
    return jax.nn.gelu(product, approximate=False).astype(jnp.bfloat16)

def layer_norm(summed):
    center = lax.optimization_barrier(jnp.mean(summed, axis=-1, keepdims=True))
    spread = lax.optimization_barrier(jnp.mean((summed - center) * (summed - center), axis=-1, keepdims=True))
    return (summed - center) * lax.rsqrt(spread + 1e-05)

def pool_units(normed, identity):
    members = (identity[None, :] == jnp.arange(SENT_DEV, dtype=jnp.int32)[:, None]).astype(jnp.float32)
    sums = jnp.dot(members, normed, precision=lax.Precision.HIGHEST)
    pooled = sums / lax.optimization_barrier(jnp.sum(members, axis=1, keepdims=True))
    return unit_rows(pooled)

def reference(tokens, sentence_ids, inner_weight, outer_weight, grid_rows, candidates, targets):

    def encode(pair):
        rows, identity = pair
        projected = jnp.dot(inner_units(rows, inner_weight), outer_weight, preferred_element_type=jnp.float32)
        normed = layer_norm(rows.astype(jnp.float32) + projected)
        return pool_units(normed, identity)
    units = lax.map(encode, (tokens.reshape(PDEV, TOK_DEV, D), sentence_ids)).reshape(NS, D)
    sources = jnp.zeros((NS, D), jnp.bfloat16).at[grid_rows].set(units)
    blocks = targets.reshape(NTB, TBLK, D)

    def listed(index):
        block = lax.dynamic_slice_in_dim(sources, index * SBLK, SBLK)
        target_units = unit_rows(blocks[candidates[index]]).reshape(K * TBLK, D)
        scores = lax.dot_general(block, target_units, (((1,), (1,)), ((), ())), preferred_element_type=jnp.float32)
        return (target_units, jnp.exp(SCORE_SCALE * scores))

    def first_pass(index):
        target_units, expo = listed(index)
        return (lax.optimization_barrier(jnp.sum(expo, axis=1)), lax.optimization_barrier(jnp.sum(expo, axis=0)).reshape(K, TBLK))
    indices = jnp.arange(NSB, dtype=jnp.int32)
    row_total, column_parts = lax.map(first_pass, indices)
    column_total = jnp.zeros((NTB, TBLK), jnp.float32).at[candidates.reshape(-1)].add(column_parts.reshape(NSB * K, TBLK))

    def second_pass(index):
        target_units, expo = listed(index)
        divisor = column_total[candidates[index]].reshape(-1)
        mutual = expo * (expo / divisor[None, :])
        numer = jnp.dot(mutual.astype(jnp.bfloat16), target_units, preferred_element_type=jnp.float32)
        mass = lax.optimization_barrier(jnp.sum(mutual, axis=1))
        square = lax.optimization_barrier(jnp.mean(numer * numer, axis=-1, keepdims=True))
        matched = (numer * lax.rsqrt(square + 1e-06)).astype(jnp.bfloat16)
        return (matched, jnp.log(mass / row_total[index]))
    matched, log_mass = lax.map(second_pass, indices)
    return (matched.reshape(NS, D), log_mass.reshape(NS))
```

```python
import math

import jax
import jax.numpy as jnp
from jax import lax
from jax.sharding import PartitionSpec as P

SENT_DEV = 32
TBLK = 256
MOST = 4


SCORE_SCALE = 32.0


def bits_of(axis, first):
    size, bit, bits = lax.axis_size(axis), first, []
    while bit < size:
        bits.append(bit)
        bit *= 2
    return bits


def swap(values, axis, offset):
    return lax.ppermute(values, axis, [(i, i ^ offset) for i in range(lax.axis_size(axis))])


def unit_rows(values):
    floats = values.astype(jnp.float32)
    square = jnp.mean(floats * floats, axis=-1, keepdims=True)
    return (floats * lax.rsqrt(square + 1e-06) * (1.0 / math.sqrt(values.shape[-1]))).astype(
        jnp.bfloat16
    )


def inner_units(rows, inner):
    product = lax.dot_general(
        rows, inner, (((1,), (1,)), ((), ())), preferred_element_type=jnp.float32
    )
    return jax.nn.gelu(product, approximate=False).astype(jnp.bfloat16)


def layer_norm(summed):
    center = jnp.mean(summed, axis=-1, keepdims=True)
    spread = jnp.mean((summed - center) * (summed - center), axis=-1, keepdims=True)
    return (summed - center) * lax.rsqrt(spread + 1e-05)


def spread_weight(weight):
    half = weight.shape[0] // 2
    near = [weight, swap(weight, "src", 2)]
    held = [lax.dynamic_slice_in_dim(weight, lax.axis_index("groups") * half, half)]
    for axis, bit in [("tgt", b) for b in bits_of("tgt", 2)] + [("src", b) for b in bits_of("src", 4)]:
        held = held + [swap(piece, axis, bit) for piece in held]
    far = []
    for piece in held[1:]:
        over_x = swap(piece, "src", 2)
        over_y = swap(piece, "groups", 1)
        far += [
            piece,
            over_x,
            over_y,
            swap(over_x[: half // 2], "groups", 1),
            swap(over_y[half // 2 :], "src", 2),
        ]
    return jnp.concatenate(near), jnp.concatenate(far)


def feed_forward(tokens, inner_weight, outer_weight):
    rows = tokens.shape[0]
    pair = jnp.concatenate([tokens, swap(tokens, "tgt", 1)])
    shared = jnp.concatenate([pair, swap(pair, "src", 1)])
    inner_near, inner_far = spread_weight(inner_weight)
    outer_near, outer_far = spread_weight(outer_weight)
    partial = jnp.dot(
        inner_units(shared, inner_near), outer_near, preferred_element_type=jnp.float32
    ) + jnp.dot(inner_units(shared, inner_far), outer_far, preferred_element_type=jnp.float32)
    other = swap(partial[2 * rows :].astype(jnp.bfloat16), "src", 1)
    chip = partial[: 2 * rows] + other.astype(jnp.float32)
    back = swap(chip[rows:].astype(jnp.bfloat16), "tgt", 1)
    return tokens.astype(jnp.float32) + chip[:rows] + back.astype(jnp.float32)


def one_hot(keys, count):
    return keys[None, :] == jnp.arange(count, dtype=jnp.int32)[:, None]


def on_device(tokens, sentence_ids, inner_weight, outer_weight, grid_rows, candidates, targets):
    features = tokens.shape[1]
    src_count = lax.axis_size("src")
    tgt_count = lax.axis_size("tgt")
    src_index = lax.axis_index("src")
    tgt_index = lax.axis_index("tgt")
    per_block = SENT_DEV // src_count
    block_rows = tgt_count * SENT_DEV

    column_blocks = targets.shape[0] // TBLK
    cand_row = candidates[0]
    listed = (cand_row // column_blocks == tgt_index).astype(jnp.int32)
    ranks = jnp.cumsum(listed) - 1
    chosen = (
        (listed[None, :] == 1) & (ranks[None, :] == jnp.arange(MOST, dtype=jnp.int32)[:, None])
    ).astype(jnp.int32)
    slot_block = jnp.sum(chosen * (cand_row % column_blocks)[None, :], axis=1)
    valid = jnp.sum(chosen, axis=1).astype(jnp.float32)
    tiles = targets.reshape(column_blocks, TBLK, features)[slot_block]
    target_units = unit_rows(tiles).reshape(MOST * TBLK, features)

    normed = layer_norm(feed_forward(tokens, inner_weight, outer_weight))
    members = one_hot(sentence_ids[0], SENT_DEV).astype(jnp.float32)
    sums = jnp.dot(members, normed, precision=lax.Precision.HIGHEST)
    unit = unit_rows(sums / jnp.sum(members, axis=1, keepdims=True))

    order_key = (grid_rows // block_rows ^ src_index) * per_block + grid_rows % per_block
    held = jnp.dot(
        one_hot(order_key, SENT_DEV).astype(jnp.bfloat16), unit, preferred_element_type=jnp.float32
    ).astype(jnp.bfloat16)
    held = held.reshape(src_count, 1, per_block, features)
    for bit in reversed(bits_of("src", 1)):
        held = jnp.concatenate([held[:bit], swap(held[bit:], "src", bit)], axis=1)
    mine = held.reshape(SENT_DEV, features)
    parts = jnp.concatenate(
        [mine] + [swap(mine, "tgt", offset) for offset in range(1, tgt_count)]
    )
    origin = jnp.arange(1, dtype=jnp.int32)
    for bit in reversed(bits_of("src", 1)):
        origin = jnp.concatenate([origin, origin ^ bit])
    from_src = (origin ^ src_index)[None, :, None]
    from_tgt = (jnp.arange(tgt_count, dtype=jnp.int32) ^ tgt_index)[:, None, None]
    place = (from_src * tgt_count + from_tgt) * per_block + jnp.arange(per_block, dtype=jnp.int32)
    block = jnp.dot(
        one_hot(place.reshape(-1), block_rows).astype(jnp.bfloat16),
        parts,
        preferred_element_type=jnp.float32,
    ).astype(jnp.bfloat16)

    scores = lax.dot_general(
        block, target_units, (((1,), (1,)), ((), ())), preferred_element_type=jnp.float32
    )
    column_valid = jnp.repeat(valid, TBLK)
    expo = jnp.exp(SCORE_SCALE * scores) * column_valid[None, :]
    row_part = jnp.sum(expo, axis=1)
    column_part = jnp.sum(expo, axis=0).reshape(MOST, TBLK)
    picker = (slot_block[:, None] == jnp.arange(column_blocks, dtype=jnp.int32)[None, :]).astype(
        jnp.float32
    )
    column_total = jnp.dot(
        (picker * valid[:, None]).T, column_part, precision=lax.Precision.HIGHEST
    )
    for bit in bits_of("src", 1):
        column_total = column_total + swap(column_total, "src", bit)
    picked = jnp.dot(picker, column_total, precision=lax.Precision.HIGHEST)
    divisor = jnp.where(valid[:, None] > 0, picked, 1.0).reshape(-1)
    mutual = expo * (expo / divisor[None, :])
    numer = jnp.dot(mutual.astype(jnp.bfloat16), target_units, preferred_element_type=jnp.float32)
    mass_part = jnp.sum(mutual, axis=1)
    sums_part = jnp.stack([mass_part, row_part])

    def rows_of(index):
        return lax.dynamic_slice_in_dim(numer, index * SENT_DEV, SENT_DEV)

    def sums_of(index):
        return lax.dynamic_slice_in_dim(sums_part, index * SENT_DEV, SENT_DEV, axis=1)

    numer_rows, sums_rows = rows_of(tgt_index), sums_of(tgt_index)
    for offset in range(1, tgt_count):
        away = tgt_index ^ offset
        numer_rows = numer_rows + swap(
            rows_of(away).astype(jnp.bfloat16), "tgt", offset
        ).astype(jnp.float32)
        sums_rows = sums_rows + swap(sums_of(away), "tgt", offset)
    square = jnp.mean(numer_rows * numer_rows, axis=-1, keepdims=True)
    matched = (numer_rows * lax.rsqrt(square + 1e-06)).astype(jnp.bfloat16)
    log_mass = jnp.log(sums_rows[0] / sums_rows[1])
    return (matched, log_mass)


def solution(mesh):
    in_specs = (
        P(("groups", "src", "tgt"), None),
        P(("groups", "src", "tgt"), None),
        P(("src", "tgt"), None),
        P(("src", "tgt"), None),
        P(("groups", "src", "tgt")),
        P(("groups", "src"), None),
        P(("groups", "tgt"), None),
    )
    out_specs = (P(("groups", "src", "tgt"), None), P(("groups", "src", "tgt")))
    return jax.shard_map(
        on_device, mesh=mesh, in_specs=in_specs, out_specs=out_specs, check_vma=False
    )
```

```python
import functools
import math

import jax
import jax.numpy as jnp
from jax import lax
from jax.experimental import pallas as pl
from jax.experimental.pallas import tpu as pltpu
from jax.sharding import PartitionSpec as P

SENT_DEV = 32
TBLK = 256
MOST = 4
LANES = 128


SCORE_SCALE = 32.0


def bits_of(axis, first):
    size, bit, bits = lax.axis_size(axis), first, []
    while bit < size:
        bits.append(bit)
        bit *= 2
    return bits


def swap(values, axis, offset):
    return lax.ppermute(values, axis, [(i, i ^ offset) for i in range(lax.axis_size(axis))])


def local_call(kernel, out_shape, args, flops, scratch=(), scalars=0):
    outs = out_shape if isinstance(out_shape, tuple) else (out_shape,)
    moved = sum(math.prod(a.shape) * a.dtype.itemsize for a in (*args, *outs))
    return pl.pallas_call(
        kernel,
        out_shape=out_shape,
        in_specs=[pl.BlockSpec(memory_space=pltpu.SMEM)] * scalars
        + [pl.BlockSpec(memory_space=pltpu.VMEM)] * (len(args) - scalars),
        out_specs=jax.tree.map(lambda _: pl.BlockSpec(memory_space=pltpu.VMEM), out_shape),
        scratch_shapes=scratch,
        compiler_params=pltpu.CompilerParams(vmem_limit_bytes=40 * 2**20),
        cost_estimate=pl.CostEstimate(flops=flops, bytes_accessed=moved, transcendentals=0),
    )(*args)


def shape(dims, dtype):
    return jax.ShapeDtypeStruct(tuple(dims), dtype)


def unit_of(floats):
    square = jnp.mean(floats * floats, axis=-1, keepdims=True)
    return (floats * lax.rsqrt(square + 1e-06) * (1.0 / math.sqrt(floats.shape[-1]))).astype(
        jnp.bfloat16
    )


def dot(left, right, contract, **more):
    return lax.dot_general(
        left, right, ((contract[:1], contract[1:]), ((), ())),
        preferred_element_type=jnp.float32, **more
    )


def gather_refs(refs, held):
    start = 0
    for ref in refs:
        held[start : start + ref.shape[0], :] = ref[...]
        start += ref.shape[0]


def hidden_kernel(count, *refs):
    tokens, weights, (out, rows, held) = refs[:count], refs[count:-3], refs[-3:]
    gather_refs(tokens, rows)
    gather_refs(weights, held)
    step = 256

    @pl.loop(0, out.shape[0] // step)
    def _(index):
        part = pl.ds(pl.multiple_of(index * step, step), step)
        product = dot(rows[part, :], held[...], (1, 1))
        out[part, :] = (
            product * 0.5 * (1.0 + lax.erf(product * math.sqrt(0.5)))
        ).astype(jnp.bfloat16)


def hidden_units(tokens, weights):
    features = weights[0].shape[1]
    rows = sum(t.shape[0] for t in tokens)
    units = sum(w.shape[0] for w in weights)
    return local_call(
        functools.partial(hidden_kernel, len(tokens)),
        shape((rows, units), jnp.bfloat16),
        (*tokens, *weights),
        2 * rows * units * features,
        (pltpu.VMEM((rows, features), jnp.bfloat16), pltpu.VMEM((units, features), jnp.bfloat16)),
    )


def partial_kernel(near_hidden, far_hidden, *refs):
    weights, (own, pair, own_sent, pair_sent, held) = refs[:-5], refs[-5:]
    gather_refs(weights, held)
    near = near_hidden.shape[1]
    rows = own.shape[0]
    for index, out in enumerate((own, pair, own_sent, pair_sent)):
        part = pl.ds(index * rows, rows)
        out[...] = (
            dot(near_hidden[part, :], held[:near, :], (1, 0))
            + dot(far_hidden[part, :], held[near:, :], (1, 0))
        ).astype(out.dtype)


def partial_sums(near_hidden, far_hidden, weights):
    rows, features = near_hidden.shape[0] // 4, weights[0].shape[1]
    units = near_hidden.shape[1] + far_hidden.shape[1]
    kept, sent = shape((rows, features), jnp.float32), shape((rows, features), jnp.bfloat16)
    return local_call(
        partial_kernel,
        (kept, kept, sent, sent),
        (near_hidden, far_hidden, *weights),
        8 * rows * units * features,
        (pltpu.VMEM((units, features), jnp.bfloat16),),
    )


def pool_kernel(count, identity, order, tokens, *refs):
    out, parts = refs[-1], refs[:-1]
    summed = []
    width = tokens.shape[1] // count
    for index in range(count):
        own, core, pair = parts[3 * index : 3 * index + 3]
        summed.append(
            tokens[:, index * width : (index + 1) * width].astype(jnp.float32)
            + (own[...] + core[...].astype(jnp.float32))
            + pair[...].astype(jnp.float32)
        )
    summed = jnp.concatenate(summed, axis=1)
    center = jnp.mean(summed, axis=-1, keepdims=True)
    moved = summed - center
    spread = jnp.mean(moved * moved, axis=-1, keepdims=True)
    normed = moved * lax.rsqrt(spread + 1e-05)
    sentences = out.shape[0]
    members = (
        identity[...] == lax.broadcasted_iota(jnp.int32, (sentences, tokens.shape[0]), 0)
    ).astype(jnp.float32)
    sums = dot(members, normed, (1, 0), precision=lax.Precision.HIGHEST)
    unit = unit_of(sums / jnp.sum(members, axis=1, keepdims=True))
    sort = (order[...] == lax.broadcasted_iota(jnp.int32, (sentences, sentences), 0)).astype(
        jnp.bfloat16
    )
    out[...] = dot(sort, unit, (1, 0)).astype(jnp.bfloat16)


def target_kernel(slots, tiles, out):
    out[...] = unit_of(tiles[...].astype(jnp.float32))


def listed_units(slot_block, targets):
    features = targets.shape[1]
    return pl.pallas_call(
        target_kernel,
        out_shape=shape((MOST * TBLK, features), jnp.bfloat16),
        grid_spec=pltpu.PrefetchScalarGridSpec(
            num_scalar_prefetch=1,
            grid=(MOST,),
            in_specs=[pl.BlockSpec((TBLK, features), lambda slot, slots: (slots[slot], 0))],
            out_specs=pl.BlockSpec((TBLK, features), lambda slot, slots: (slot, 0)),
        ),
        compiler_params=pltpu.CompilerParams(vmem_limit_bytes=40 * 2**20),
        cost_estimate=pl.CostEstimate(
            flops=8 * MOST * TBLK * features,
            bytes_accessed=4 * MOST * TBLK * features,
            transcendentals=0,
        ),
    )(slot_block, targets)


def score_kernel(slots, valid, place, units, *refs):
    parts, (expo, columns, row_total, held) = refs[:-4], refs[-4:]
    gather_refs(parts, held)
    rows = expo.shape[0]
    sort = (place[...] == lax.broadcasted_iota(jnp.int32, (rows, rows), 0)).astype(jnp.bfloat16)
    block = dot(sort, held[...], (1, 0)).astype(jnp.bfloat16)
    columns[...] = jnp.zeros_like(columns)
    total = jnp.zeros((rows, 1), jnp.float32)
    for slot in range(MOST):
        part = pl.ds(slot * TBLK, TBLK)
        weight = valid[slot].astype(jnp.float32)
        values = jnp.exp(SCORE_SCALE * dot(block, units[part, :], (1, 1))) * weight
        expo[:, part] = values
        total = total + jnp.sum(values, axis=1, keepdims=True)
        column = jnp.sum(values, axis=0, keepdims=True)

        @pl.when(valid[slot] > 0)
        def _():
            columns[pl.ds(slots[slot], 1), :] = column

    row_total[...] = total


def extra_columns(values):
    lane = lax.broadcasted_iota(jnp.int32, (values[0].shape[0], LANES), 1)
    out = jnp.zeros(lane.shape, jnp.float32)
    for index, value in enumerate(values):
        out = jnp.where(lane == index, value, out)
    return out


def thirds(value):
    first = value.astype(jnp.bfloat16).astype(jnp.float32)
    second = (value - first).astype(jnp.bfloat16).astype(jnp.float32)
    return [first, second, value - first - second]


def match_kernel(slots, valid, expo, columns, row_total, units, own, sent):
    rows = own.shape[0]
    features = units.shape[1]
    mass = jnp.zeros((expo.shape[0], 1), jnp.float32)
    weights = []
    for slot in range(MOST):
        part = pl.ds(slot * TBLK, TBLK)
        values = expo[:, part]
        listed = valid[slot].astype(jnp.float32)
        divisor = jnp.where(listed > 0, columns[pl.ds(slots[slot], 1), :], 1.0)
        mutual = values * (values / divisor)
        mass = mass + jnp.sum(mutual, axis=1, keepdims=True)
        weights.append(mutual.astype(jnp.bfloat16))
    numer = dot(jnp.concatenate(weights, axis=1), units[...], (1, 0))
    totals = row_total[...]
    zero = jnp.zeros((rows, 1), jnp.float32)
    own[:, :features] = numer[:rows]
    own[:, features:] = extra_columns([mass[:rows], zero, zero, totals[:rows]])
    sent[:, :features] = numer[rows:].astype(jnp.bfloat16)
    sent[:, features:] = extra_columns(thirds(mass[rows:]) + thirds(totals[rows:])).astype(
        jnp.bfloat16
    )


def finish_kernel(own, *refs):
    parts, (matched, log_mass) = refs[:-2], refs[-2:]
    rows, features = matched.shape
    total = own[...]
    for part in parts:
        total = total + part[...].astype(jnp.float32)
    numer = total[:, :features]
    square = jnp.mean(numer * numer, axis=-1, keepdims=True)
    matched[...] = (numer * lax.rsqrt(square + 1e-06)).astype(jnp.bfloat16)
    extra = total[:, features:]
    lane = lax.broadcasted_iota(jnp.int32, extra.shape, 1)
    mass = jnp.sum(jnp.where(lane < 3, extra, 0.0), axis=1, keepdims=True)
    whole = jnp.sum(jnp.where(lane < 3, 0.0, extra), axis=1, keepdims=True)
    ratio = mass / whole
    same = lax.broadcasted_iota(jnp.int32, (rows, rows), 0) == lax.broadcasted_iota(
        jnp.int32, (rows, rows), 1
    )
    log_mass[...] = jnp.log(jnp.sum(jnp.where(same, ratio, 0.0), axis=0, keepdims=True))


def over_square(piece):
    half = piece.shape[0] // 2 // 16 * 16
    over_x = swap(piece, "src", 2)
    over_y = swap(piece, "groups", 1)
    return [
        piece,
        over_x,
        over_y,
        swap(over_x[:half], "groups", 1),
        swap(over_y[half:], "src", 2),
    ]


def far_pieces(half):
    held = half
    for axis, bit in [("tgt", b) for b in bits_of("tgt", 2)] + [("src", b) for b in bits_of("src", 4)]:
        held = jnp.concatenate([held, swap(held, axis, bit)])
    return held[half.shape[0] :]


def feed_forward(tokens, inner_weight, outer_weight, other_work):
    units, features = inner_weight.shape
    half = units // 2
    start = lax.axis_index("groups") * half
    inner_half = lax.dynamic_slice_in_dim(inner_weight, start, half)
    outer_half = lax.dynamic_slice_in_dim(outer_weight, start, half)
    inner_far = over_square(far_pieces(inner_half))
    near_sent = jnp.concatenate([inner_half, outer_half])
    near_x = swap(near_sent, "src", 2)
    near_y = swap(near_x, "groups", 1)
    outer_half, other_work = lax.optimization_barrier((outer_half, other_work))
    columns = 2
    width = features // columns
    outer_far = [
        over_square(far_pieces(outer_half[:, c * width : (c + 1) * width])) for c in range(columns)
    ]
    neighbour = swap(tokens, "tgt", 1)
    shared = [tokens, neighbour, swap(tokens, "src", 1), swap(neighbour, "src", 1)]
    near_hidden = hidden_units(shared, [inner_weight, near_x[:half], near_y[:half]])
    far_hidden = hidden_units(shared, inner_far)
    summands = []
    for c in range(columns):
        near = [
            w[:, c * width : (c + 1) * width]
            for w in (outer_weight, near_x[half:], near_y[half:])
        ]
        own, pair, own_sent, pair_sent = partial_sums(near_hidden, far_hidden, near + outer_far[c])
        pair = pair + swap(pair_sent, "src", 1).astype(jnp.float32)
        summands += [own, swap(own_sent, "src", 1), swap(pair.astype(jnp.bfloat16), "tgt", 1)]
    return summands, other_work


def on_device(tokens, sentence_ids, inner_weight, outer_weight, grid_rows, candidates, targets):
    features = tokens.shape[1]
    src_count = lax.axis_size("src")
    tgt_count = lax.axis_size("tgt")
    src_index = lax.axis_index("src")
    tgt_index = lax.axis_index("tgt")
    per_block = SENT_DEV // src_count
    block_rows = tgt_count * SENT_DEV

    column_blocks = targets.shape[0] // TBLK
    cand_row = candidates[0]
    listed = (cand_row // column_blocks == tgt_index).astype(jnp.int32)
    ranks = jnp.cumsum(listed) - 1
    chosen = (
        (listed[None, :] == 1) & (ranks[None, :] == jnp.arange(MOST, dtype=jnp.int32)[:, None])
    ).astype(jnp.int32)
    slot_block = jnp.sum(chosen * (cand_row % column_blocks)[None, :], axis=1)
    valid = jnp.sum(chosen, axis=1)
    target_units = listed_units(slot_block, targets)

    summands, target_units = feed_forward(tokens, inner_weight, outer_weight, target_units)
    order_key = (grid_rows // block_rows ^ src_index) * per_block + grid_rows % per_block
    held = local_call(
        functools.partial(pool_kernel, len(summands) // 3),
        shape((SENT_DEV, features), jnp.bfloat16),
        (sentence_ids, order_key.reshape(1, -1), tokens, *summands),
        20 * tokens.shape[0] * features,
    )
    held = held.reshape(src_count, 1, per_block, features)
    for bit in reversed(bits_of("src", 1)):
        held = jnp.concatenate([held[:bit], swap(held[bit:], "src", bit)], axis=1)
    mine = held.reshape(SENT_DEV, features)
    parts = [mine] + [swap(mine, "tgt", offset) for offset in range(1, tgt_count)]
    origin = jnp.arange(1, dtype=jnp.int32)
    for bit in reversed(bits_of("src", 1)):
        origin = jnp.concatenate([origin, origin ^ bit])
    from_src = (origin ^ src_index)[None, :, None]
    from_tgt = (jnp.arange(tgt_count, dtype=jnp.int32) ^ tgt_index)[:, None, None]
    place = (from_src * tgt_count + from_tgt) * per_block + jnp.arange(per_block, dtype=jnp.int32)
    place = place.reshape(1, -1) ^ (tgt_index * SENT_DEV)

    pairs = MOST * TBLK
    expo, column_total, row_total = local_call(
        score_kernel,
        (
            shape((block_rows, pairs), jnp.float32),
            shape((column_blocks, TBLK), jnp.float32),
            shape((block_rows, 1), jnp.float32),
        ),
        (slot_block, valid, place, target_units, *parts),
        2 * block_rows * pairs * features,
        (pltpu.VMEM((block_rows, features), jnp.bfloat16),),
        scalars=2,
    )
    for bit in bits_of("src", 1):
        column_total = column_total + swap(column_total, "src", bit)
    own, sent = local_call(
        match_kernel,
        (
            shape((SENT_DEV, features + LANES), jnp.float32),
            shape((block_rows - SENT_DEV, features + LANES), jnp.bfloat16),
        ),
        (slot_block, valid, expo, column_total, row_total, target_units),
        2 * block_rows * pairs * features,
        scalars=2,
    )
    received = [
        swap(sent[(offset - 1) * SENT_DEV : offset * SENT_DEV], "tgt", offset)
        for offset in range(1, tgt_count)
    ]
    matched, log_mass = local_call(
        finish_kernel,
        (shape((SENT_DEV, features), jnp.bfloat16), shape((1, SENT_DEV), jnp.float32)),
        (own, *received),
        8 * SENT_DEV * features,
    )
    return (matched, log_mass.reshape(SENT_DEV))


def solution(mesh):
    in_specs = (
        P(("groups", "src", "tgt"), None),
        P(("groups", "src", "tgt"), None),
        P(("src", "tgt"), None),
        P(("src", "tgt"), None),
        P(("groups", "src", "tgt")),
        P(("groups", "src"), None),
        P(("groups", "tgt"), None),
    )
    out_specs = (P(("groups", "src", "tgt"), None), P(("groups", "src", "tgt")))
    return jax.shard_map(
        on_device, mesh=mesh, in_specs=in_specs, out_specs=out_specs, check_vma=False
    )
```

```python
import functools
import math

import jax
import jax.numpy as jnp
from jax import lax
from jax.experimental import pallas as pl
from jax.experimental.pallas import tpu as pltpu
from jax.sharding import PartitionSpec as P

SENT_DEV = 32
TBLK = 256
MOST = 4
LANES = 128


SCORE_SCALE = 32.0


def bits_of(axis, first):
    size, bit, bits = lax.axis_size(axis), first, []
    while bit < size:
        bits.append(bit)
        bit *= 2
    return bits


def swap(values, axis, offset):
    return lax.ppermute(values, axis, [(i, i ^ offset) for i in range(lax.axis_size(axis))])


def local_call(
    kernel, out_shape, args, flops, scratch=(), scalars=0, near=0, place=pltpu.VMEM, vmem=16
):
    outs = out_shape if isinstance(out_shape, tuple) else (out_shape,)
    moved = sum(math.prod(a.shape) * a.dtype.itemsize for a in (*args, *outs))
    return pl.pallas_call(
        kernel,
        out_shape=out_shape,
        in_specs=[pl.BlockSpec(memory_space=pltpu.SMEM)] * scalars
        + [pl.BlockSpec(memory_space=pltpu.VMEM)] * near
        + [pl.BlockSpec(memory_space=place)] * (len(args) - scalars - near),
        out_specs=jax.tree.map(lambda _: pl.BlockSpec(memory_space=pltpu.VMEM), out_shape),
        scratch_shapes=scratch,
        compiler_params=pltpu.CompilerParams(vmem_limit_bytes=vmem * 2**20),
        cost_estimate=pl.CostEstimate(flops=flops, bytes_accessed=moved, transcendentals=0),
    )(*args)


def shape(dims, dtype):
    return jax.ShapeDtypeStruct(tuple(dims), dtype)


def unit_of(floats):
    square = jnp.mean(floats * floats, axis=-1, keepdims=True)
    return (floats * lax.rsqrt(square + 1e-06) * (1.0 / math.sqrt(floats.shape[-1]))).astype(
        jnp.bfloat16
    )


def dot(left, right, contract, **more):
    return lax.dot_general(
        left, right, ((contract[:1], contract[1:]), ((), ())),
        preferred_element_type=jnp.float32, **more
    )


def gather_refs(refs, held):
    start = 0
    for ref in refs:
        held[start : start + ref.shape[0], :] = ref[...]
        start += ref.shape[0]


def fetches(refs, held, sems):
    start, copies = 0, []
    for index, ref in enumerate(refs):
        count = ref.shape[0]
        copies.append(
            pltpu.make_async_copy(ref, held.at[pl.ds(start, count)], sems.at[index])
        )
        start += count
    for copy in copies:
        copy.start()
    return copies


def slice_kernel(inner, outer, inner_half, outer_half, sems):
    half = inner_half.shape[0]
    rows = pl.ds(pl.multiple_of(lax.axis_index("groups") * half, half), half)
    copies = [
        pltpu.make_async_copy(inner.at[rows], inner_half, sems.at[0]),
        pltpu.make_async_copy(outer.at[rows], outer_half, sems.at[1]),
    ]
    for copy in copies:
        copy.start()
    for copy in copies:
        copy.wait()


def weight_halves(inner, outer):
    units, features = inner.shape
    return local_call(
        slice_kernel,
        (shape((units // 2, features), jnp.bfloat16),) * 2,
        (inner, outer),
        0,
        (pltpu.SemaphoreType.DMA((2,)),),
        place=pl.ANY,
        vmem=58,
    )


def hidden_kernel(count, *refs):
    tokens, weights = refs[:count], refs[count:-5]
    out, rows, held, token_sems, weight_sems = refs[-5:]
    weight_copies = fetches(weights, held, weight_sems)
    token_copies = fetches(tokens, rows, token_sems)
    for copy in weight_copies:
        copy.wait()
    start = 0
    for token, copy in zip(tokens, token_copies):
        part = pl.ds(start, token.shape[0])
        copy.wait()
        product = dot(rows[part, :], held[...], (1, 1))
        out[part, :] = (
            product * 0.5 * (1.0 + lax.erf(product * math.sqrt(0.5)))
        ).astype(jnp.bfloat16)
        start += token.shape[0]


def hidden_units(tokens, weights):
    features = weights[0].shape[1]
    rows = sum(t.shape[0] for t in tokens)
    units = sum(w.shape[0] for w in weights)
    return local_call(
        functools.partial(hidden_kernel, len(tokens)),
        shape((rows, units), jnp.bfloat16),
        (*tokens, *weights),
        2 * rows * units * features,
        (
            pltpu.VMEM((rows, features), jnp.bfloat16),
            pltpu.VMEM((units, features), jnp.bfloat16),
            pltpu.SemaphoreType.DMA((len(tokens),)),
            pltpu.SemaphoreType.DMA((len(weights),)),
        ),
        place=pl.ANY,
    )


def partial_kernel(blocks, added, hidden, *refs):
    terms, refs = refs[:added], refs[added:]
    weights, outs, (held, sems) = refs[: -len(blocks) - 2], refs[-len(blocks) - 2 : -2], refs[-2:]
    for copy in fetches(weights, held, sems):
        copy.wait()
    for index, out in zip(blocks, outs):
        rows = out.shape[0]
        sums = dot(hidden[pl.ds(index * rows, rows), :], held[...], (1, 0))
        for term in terms:
            sums = sums + term[...].astype(jnp.float32)
        out[...] = sums.astype(out.dtype)


def partial_sums(hidden, weights, blocks, terms=(), dtype=jnp.bfloat16):
    rows, units, features = hidden.shape[0] // 4, hidden.shape[1], weights[0].shape[1]
    return local_call(
        functools.partial(partial_kernel, blocks, len(terms)),
        (shape((rows, features), dtype),) * len(blocks),
        (hidden, *terms, *weights),
        2 * len(blocks) * rows * units * features,
        (
            pltpu.VMEM((units, features), jnp.bfloat16),
            pltpu.SemaphoreType.DMA((len(weights),)),
        ),
        near=1 + len(terms),
        place=pl.ANY,
    )


def pool_kernel(identity, order, own, back, out):
    summed = own[...] + back[...].astype(jnp.float32)
    center = jnp.mean(summed, axis=-1, keepdims=True)
    moved = summed - center
    spread = jnp.mean(moved * moved, axis=-1, keepdims=True)
    normed = moved * lax.rsqrt(spread + 1e-05)
    sentences = out.shape[0]
    members = (
        identity[...] == lax.broadcasted_iota(jnp.int32, (sentences, own.shape[0]), 0)
    ).astype(jnp.float32)
    sums = dot(members, normed, (1, 0), precision=lax.Precision.HIGHEST)
    unit = unit_of(sums / jnp.sum(members, axis=1, keepdims=True))
    sort = (order[...] == lax.broadcasted_iota(jnp.int32, (sentences, sentences), 0)).astype(
        jnp.bfloat16
    )
    out[...] = dot(sort, unit, (1, 0)).astype(jnp.bfloat16)


def find_slots(listed, slots, valid, blocks):
    column = lax.axis_index("tgt")
    for slot in range(MOST):
        slots[slot] = 0
        valid[slot] = 0
    count = jnp.int32(0)
    for index in range(listed.shape[1]):
        block = listed[0, index]
        here = lax.div(block, blocks) == column

        @pl.when(here)
        def _():
            slots[count] = lax.rem(block, blocks)
            valid[count] = 1

        count = count + here.astype(jnp.int32)


SLOTS = (pltpu.SMEM((MOST,), jnp.int32),) * 2


def target_kernel(listed, targets, out, slots, valid, tiles, sems):
    find_slots(listed, slots, valid, targets.shape[0] // TBLK)
    copies = [
        pltpu.make_async_copy(
            targets.at[pl.ds(pl.multiple_of(slots[slot] * TBLK, TBLK), TBLK)],
            tiles.at[slot],
            sems.at[slot],
        )
        for slot in range(MOST)
    ]
    for copy in copies:
        copy.start()
    for slot, copy in enumerate(copies):
        copy.wait()
        out[slot * TBLK : (slot + 1) * TBLK, :] = unit_of(tiles[slot].astype(jnp.float32))


def listed_units(candidates, targets):
    features = targets.shape[1]
    return local_call(
        target_kernel,
        shape((MOST * TBLK, features), jnp.bfloat16),
        (candidates, targets),
        8 * MOST * TBLK * features,
        (
            *SLOTS,
            pltpu.VMEM((MOST, TBLK, features), jnp.bfloat16),
            pltpu.SemaphoreType.DMA((MOST,)),
        ),
        scalars=1,
        place=pl.ANY,
        vmem=58,
    )


def score_kernel(listed, place, *refs):
    parts, (units_ref, expo, columns, row_total, slots, valid, units, held, sems) = (
        refs[:-9],
        refs[-9:],
    )
    copies = [
        pltpu.make_async_copy(
            units_ref.at[pl.ds(slot * TBLK, TBLK)], units.at[slot], sems.at[slot]
        )
        for slot in range(MOST)
    ]
    for copy in copies:
        copy.start()
    find_slots(listed, slots, valid, columns.shape[0])
    gather_refs(parts, held)
    rows = expo.shape[0]
    sort = (place[...] == lax.broadcasted_iota(jnp.int32, (rows, rows), 0)).astype(jnp.bfloat16)
    block = dot(sort, held[...], (1, 0)).astype(jnp.bfloat16)
    columns[...] = jnp.zeros_like(columns)
    total = jnp.zeros((rows, 1), jnp.float32)
    for slot in range(MOST):
        part = pl.ds(slot * TBLK, TBLK)
        weight = valid[slot].astype(jnp.float32)
        copies[slot].wait()
        values = jnp.exp(SCORE_SCALE * dot(block, units[slot], (1, 1))) * weight
        expo[:, part] = values
        total = total + jnp.sum(values, axis=1, keepdims=True)
        column = jnp.sum(values, axis=0, keepdims=True)

        @pl.when(valid[slot] > 0)
        def _():
            columns[pl.ds(slots[slot], 1), :] = column

    row_total[...] = total


def extra_columns(values):
    lane = lax.broadcasted_iota(jnp.int32, (values[0].shape[0], LANES), 1)
    out = jnp.zeros(lane.shape, jnp.float32)
    for index, value in enumerate(values):
        out = jnp.where(lane == index, value, out)
    return out


def thirds(value):
    first = value.astype(jnp.bfloat16).astype(jnp.float32)
    second = (value - first).astype(jnp.bfloat16).astype(jnp.float32)
    return [first, second, value - first - second]


def match_kernel(listed, expo, columns, row_total, units_ref, own, sent, slots, valid, units, sem):
    copy = pltpu.make_async_copy(units_ref, units, sem)
    copy.start()
    find_slots(listed, slots, valid, columns.shape[0])
    rows = own.shape[0]
    features = units.shape[1]
    mass = jnp.zeros((expo.shape[0], 1), jnp.float32)
    weights = []
    for slot in range(MOST):
        part = pl.ds(slot * TBLK, TBLK)
        values = expo[:, part]
        listed = valid[slot].astype(jnp.float32)
        divisor = jnp.where(listed > 0, columns[pl.ds(slots[slot], 1), :], 1.0)
        mutual = values * (values / divisor)
        mass = mass + jnp.sum(mutual, axis=1, keepdims=True)
        weights.append(mutual.astype(jnp.bfloat16))
    copy.wait()
    numer = dot(jnp.concatenate(weights, axis=1), units[...], (1, 0))
    totals = row_total[...]
    zero = jnp.zeros((rows, 1), jnp.float32)
    own[:, :features] = numer[:rows]
    own[:, features:] = extra_columns([mass[:rows], zero, zero, totals[:rows]])
    sent[:, :features] = numer[rows:].astype(jnp.bfloat16)
    sent[:, features:] = extra_columns(thirds(mass[rows:]) + thirds(totals[rows:])).astype(
        jnp.bfloat16
    )


def finish_kernel(own, *refs):
    parts, (matched, log_mass) = refs[:-2], refs[-2:]
    rows, features = matched.shape
    total = own[...]
    for part in parts:
        total = total + part[...].astype(jnp.float32)
    numer = total[:, :features]
    square = jnp.mean(numer * numer, axis=-1, keepdims=True)
    matched[...] = (numer * lax.rsqrt(square + 1e-06)).astype(jnp.bfloat16)
    extra = total[:, features:]
    lane = lax.broadcasted_iota(jnp.int32, extra.shape, 1)
    mass = jnp.sum(jnp.where(lane < 3, extra, 0.0), axis=1, keepdims=True)
    whole = jnp.sum(jnp.where(lane < 3, 0.0, extra), axis=1, keepdims=True)
    ratio = mass / whole
    same = lax.broadcasted_iota(jnp.int32, (rows, rows), 0) == lax.broadcasted_iota(
        jnp.int32, (rows, rows), 1
    )
    log_mass[...] = jnp.log(jnp.sum(jnp.where(same, ratio, 0.0), axis=0, keepdims=True))


def far_piece(half):
    held = half
    for axis, bit in [("tgt", b) for b in bits_of("tgt", 2)] + [("src", b) for b in bits_of("src", 4)]:
        held = jnp.concatenate([held, swap(held, axis, bit)])
    return held[half.shape[0] :]


def feed_forward(tokens, inner_weight, outer_weight):
    barrier = lax.optimization_barrier
    inner_x, outer_x = swap(inner_weight, "src", 2), swap(outer_weight, "src", 2)
    inner_half, outer_half = weight_halves(inner_weight, outer_weight)
    inner_far, outer_far = far_piece(inner_half), far_piece(outer_half)
    tokens_sent, inner_x = barrier((tokens, inner_x))
    neighbour = swap(tokens_sent, "tgt", 1)
    inner_far_x, inner_far_y = swap(inner_far, "src", 2), swap(inner_far, "groups", 1)

    outer_far, inner_far_x, inner_far_y, outer_x, neighbour = barrier(
        (outer_far, inner_far_x, inner_far_y, outer_x, neighbour)
    )
    outer_far_x, outer_far_y = swap(outer_far, "src", 2), swap(outer_far, "groups", 1)
    inner_square = [inner_far_x, inner_far_y, swap(inner_far_y, "src", 2)]
    outer_square = [outer_far_x, outer_far_y, swap(outer_far_x, "groups", 1)]
    shared = [tokens, neighbour, swap(tokens, "src", 1), swap(neighbour, "src", 1)]
    hidden = hidden_units(shared, [inner_weight, inner_x, inner_far, *inner_square])
    hidden, outer_square = barrier((hidden, outer_square))

    weights = [outer_weight, outer_x, outer_far, *outer_square]
    pair, own = partial_sums(hidden, weights, (3, 2))
    pair, own = swap(pair, "src", 1), swap(own, "src", 1)
    (back,) = partial_sums(hidden, weights, (1,), (pair,))
    back, hidden = barrier((back, hidden))
    back = swap(back, "tgt", 1)
    (own,) = partial_sums(hidden, weights, (0,), (tokens, own), jnp.float32)
    return own, back


def on_device(tokens, sentence_ids, inner_weight, outer_weight, grid_rows, candidates, targets):
    features = tokens.shape[1]
    src_count = lax.axis_size("src")
    tgt_count = lax.axis_size("tgt")
    src_index = lax.axis_index("src")
    tgt_index = lax.axis_index("tgt")
    per_block = SENT_DEV // src_count
    block_rows = tgt_count * SENT_DEV

    column_blocks = targets.shape[0] // TBLK
    target_units = listed_units(candidates, targets)

    summands = feed_forward(tokens, inner_weight, outer_weight)
    order_key = (grid_rows // block_rows ^ src_index) * per_block + grid_rows % per_block
    held = local_call(
        pool_kernel,
        shape((SENT_DEV, features), jnp.bfloat16),
        (sentence_ids, order_key.reshape(1, -1), *summands),
        20 * tokens.shape[0] * features,
    )
    held = held.reshape(src_count, 1, per_block, features)
    for bit in reversed(bits_of("src", 1)):
        held = jnp.concatenate([held[:bit], swap(held[bit:], "src", bit)], axis=1)
    mine = held.reshape(SENT_DEV, features)
    parts = [mine] + [swap(mine, "tgt", offset) for offset in range(1, tgt_count)]
    origin = jnp.arange(1, dtype=jnp.int32)
    for bit in reversed(bits_of("src", 1)):
        origin = jnp.concatenate([origin, origin ^ bit])
    from_src = (origin ^ src_index)[None, :, None]
    from_tgt = (jnp.arange(tgt_count, dtype=jnp.int32) ^ tgt_index)[:, None, None]
    place = (from_src * tgt_count + from_tgt) * per_block + jnp.arange(per_block, dtype=jnp.int32)
    place = place.reshape(1, -1) ^ (tgt_index * SENT_DEV)

    pairs = MOST * TBLK
    expo, column_total, row_total = local_call(
        score_kernel,
        (
            shape((block_rows, pairs), jnp.float32),
            shape((column_blocks, TBLK), jnp.float32),
            shape((block_rows, 1), jnp.float32),
        ),
        (candidates, place, *parts, target_units),
        2 * block_rows * pairs * features,
        (
            *SLOTS,
            pltpu.VMEM((MOST, TBLK, features), jnp.bfloat16),
            pltpu.VMEM((block_rows, features), jnp.bfloat16),
            pltpu.SemaphoreType.DMA((MOST,)),
        ),
        scalars=1,
        near=1 + len(parts),
        place=pl.ANY,
    )
    for bit in bits_of("src", 1):
        column_total = column_total + swap(column_total, "src", bit)
    own, sent = local_call(
        match_kernel,
        (
            shape((SENT_DEV, features + LANES), jnp.float32),
            shape((block_rows - SENT_DEV, features + LANES), jnp.bfloat16),
        ),
        (candidates, expo, column_total, row_total, target_units),
        2 * block_rows * pairs * features,
        (
            *SLOTS,
            pltpu.VMEM((MOST * TBLK, features), jnp.bfloat16),
            pltpu.SemaphoreType.DMA(()),
        ),
        scalars=1,
        near=3,
        place=pl.ANY,
    )
    received = [
        swap(sent[(offset - 1) * SENT_DEV : offset * SENT_DEV], "tgt", offset)
        for offset in range(1, tgt_count)
    ]
    matched, log_mass = local_call(
        finish_kernel,
        (shape((SENT_DEV, features), jnp.bfloat16), shape((1, SENT_DEV), jnp.float32)),
        (own, *received),
        8 * SENT_DEV * features,
    )
    return (matched, log_mass.reshape(SENT_DEV))


def solution(mesh):
    in_specs = (
        P(("groups", "src", "tgt"), None),
        P(("groups", "src", "tgt"), None),
        P(("src", "tgt"), None),
        P(("src", "tgt"), None),
        P(("groups", "src", "tgt")),
        P(("groups", "src"), None),
        P(("groups", "tgt"), None),
    )
    out_specs = (P(("groups", "src", "tgt"), None), P(("groups", "src", "tgt")))
    return jax.shard_map(
        on_device, mesh=mesh, in_specs=in_specs, out_specs=out_specs, check_vma=False
    )
```

```python
import functools
import math

import jax
import jax.numpy as jnp
from jax import lax
from jax.experimental import pallas as pl
from jax.experimental.pallas import tpu as pltpu
from jax.sharding import PartitionSpec as P

SENT_DEV = 32
TBLK = 256
MOST = 4
LANES = 128


SCORE_SCALE = 32.0


def bits_of(axis, first):
    size, bit, bits = lax.axis_size(axis), first, []
    while bit < size:
        bits.append(bit)
        bit *= 2
    return bits


def swap(values, axis, offset):
    return lax.ppermute(values, axis, [(i, i ^ offset) for i in range(lax.axis_size(axis))])


def local_call(
    kernel, out_shape, args, flops, scratch=(), scalars=0, near=0, place=pltpu.VMEM, vmem=16
):
    outs = out_shape if isinstance(out_shape, tuple) else (out_shape,)
    moved = sum(math.prod(a.shape) * a.dtype.itemsize for a in (*args, *outs))
    return pl.pallas_call(
        kernel,
        out_shape=out_shape,
        in_specs=[pl.BlockSpec(memory_space=pltpu.SMEM)] * scalars
        + [pl.BlockSpec(memory_space=pltpu.VMEM)] * near
        + [pl.BlockSpec(memory_space=place)] * (len(args) - scalars - near),
        out_specs=jax.tree.map(lambda _: pl.BlockSpec(memory_space=pltpu.VMEM), out_shape),
        scratch_shapes=scratch,
        compiler_params=pltpu.CompilerParams(vmem_limit_bytes=vmem * 2**20),
        cost_estimate=pl.CostEstimate(flops=flops, bytes_accessed=moved, transcendentals=0),
    )(*args)


def shape(dims, dtype):
    return jax.ShapeDtypeStruct(tuple(dims), dtype)


def unit_of(floats):
    square = jnp.mean(floats * floats, axis=-1, keepdims=True)
    return (floats * lax.rsqrt(square + 1e-06) * (1.0 / math.sqrt(floats.shape[-1]))).astype(
        jnp.bfloat16
    )


def dot(left, right, contract, **more):
    return lax.dot_general(
        left, right, ((contract[:1], contract[1:]), ((), ())),
        preferred_element_type=jnp.float32, **more
    )


def gather_refs(refs, held):
    start = 0
    for ref in refs:
        held[start : start + ref.shape[0], :] = ref[...]
        start += ref.shape[0]


def fetches(refs, held, sems):
    start, copies = 0, []
    for index, ref in enumerate(refs):
        count = ref.shape[0]
        copies.append(
            pltpu.make_async_copy(ref, held.at[pl.ds(start, count)], sems.at[index])
        )
        start += count
    for copy in copies:
        copy.start()
    return copies


def slice_kernel(inner, outer, inner_half, outer_half, sems):
    half = inner_half.shape[0]
    rows = pl.ds(pl.multiple_of(lax.axis_index("groups") * half, half), half)
    copies = [
        pltpu.make_async_copy(inner.at[rows], inner_half, sems.at[0]),
        pltpu.make_async_copy(outer.at[rows], outer_half, sems.at[1]),
    ]
    for copy in copies:
        copy.start()
    for copy in copies:
        copy.wait()


def weight_halves(inner, outer):
    units, features = inner.shape
    return local_call(
        slice_kernel,
        (shape((units // 2, features), jnp.bfloat16),) * 2,
        (inner, outer),
        0,
        (pltpu.SemaphoreType.DMA((2,)),),
        place=pl.ANY,
        vmem=58,
    )


def hidden_kernel(count, *refs):
    tokens, weights = refs[:count], refs[count:-5]
    out, rows, held, token_sems, weight_sems = refs[-5:]
    weight_copies = fetches(weights, held, weight_sems)
    token_copies = fetches(tokens, rows, token_sems)
    for copy in weight_copies:
        copy.wait()
    start = 0
    for token, copy in zip(tokens, token_copies):
        part = pl.ds(start, token.shape[0])
        copy.wait()
        product = dot(rows[part, :], held[...], (1, 1))
        out[part, :] = (
            product * 0.5 * (1.0 + lax.erf(product * math.sqrt(0.5)))
        ).astype(jnp.bfloat16)
        start += token.shape[0]


def hidden_units(tokens, weights):
    features = weights[0].shape[1]
    rows = sum(t.shape[0] for t in tokens)
    units = sum(w.shape[0] for w in weights)
    return local_call(
        functools.partial(hidden_kernel, len(tokens)),
        shape((rows, units), jnp.bfloat16),
        (*tokens, *weights),
        2 * rows * units * features,
        (
            pltpu.VMEM((rows, features), jnp.bfloat16),
            pltpu.VMEM((units, features), jnp.bfloat16),
            pltpu.SemaphoreType.DMA((len(tokens),)),
            pltpu.SemaphoreType.DMA((len(weights),)),
        ),
        place=pl.ANY,
    )


def partial_kernel(blocks, added, near, far, *refs):
    terms, refs = refs[:added], refs[added:]
    split = near.shape[1]
    weights, outs, (held, sems) = refs[: -len(blocks) - 2], refs[-len(blocks) - 2 : -2], refs[-2:]
    for copy in fetches(weights, held, sems):
        copy.wait()
    for index, out in zip(blocks, outs):
        rows = out.shape[0]
        part = pl.ds(index * rows, rows)
        sums = dot(near[part, :], held[:split, :], (1, 0)) + dot(far[part, :], held[split:, :], (1, 0))
        for term in terms:
            sums = sums + term[...].astype(jnp.float32)
        out[...] = sums.astype(out.dtype)


def partial_sums(hidden, weights, blocks, terms=(), dtype=jnp.bfloat16):
    rows, features = hidden[0].shape[0] // 4, weights[0].shape[1]
    units = hidden[0].shape[1] + hidden[1].shape[1]
    return local_call(
        functools.partial(partial_kernel, blocks, len(terms)),
        (shape((rows, features), dtype),) * len(blocks),
        (*hidden, *terms, *weights),
        2 * len(blocks) * rows * units * features,
        (
            pltpu.VMEM((units, features), jnp.bfloat16),
            pltpu.SemaphoreType.DMA((len(weights),)),
        ),
        near=2 + len(terms),
        place=pl.ANY,
    )


def pool_kernel(identity, order, own, back, out):
    summed = own[...] + back[...].astype(jnp.float32)
    center = jnp.mean(summed, axis=-1, keepdims=True)
    moved = summed - center
    spread = jnp.mean(moved * moved, axis=-1, keepdims=True)
    normed = moved * lax.rsqrt(spread + 1e-05)
    sentences = out.shape[0]
    members = (
        identity[...] == lax.broadcasted_iota(jnp.int32, (sentences, own.shape[0]), 0)
    ).astype(jnp.float32)
    sums = dot(members, normed, (1, 0), precision=lax.Precision.HIGHEST)
    unit = unit_of(sums / jnp.sum(members, axis=1, keepdims=True))
    sort = (order[...] == lax.broadcasted_iota(jnp.int32, (sentences, sentences), 0)).astype(
        jnp.bfloat16
    )
    out[...] = dot(sort, unit, (1, 0)).astype(jnp.bfloat16)


def find_slots(listed, slots, valid, blocks):
    column = lax.axis_index("tgt")
    for slot in range(MOST):
        slots[slot] = 0
        valid[slot] = 0
    count = jnp.int32(0)
    for index in range(listed.shape[1]):
        block = listed[0, index]
        here = lax.div(block, blocks) == column

        @pl.when(here)
        def _():
            slots[count] = lax.rem(block, blocks)
            valid[count] = 1

        count = count + here.astype(jnp.int32)


SLOTS = (pltpu.SMEM((MOST,), jnp.int32),) * 2


def target_kernel(listed, targets, out, slots, valid, tiles, sems):
    find_slots(listed, slots, valid, targets.shape[0] // TBLK)
    copies = [
        pltpu.make_async_copy(
            targets.at[pl.ds(pl.multiple_of(slots[slot] * TBLK, TBLK), TBLK)],
            tiles.at[slot],
            sems.at[slot],
        )
        for slot in range(MOST)
    ]
    for copy in copies:
        copy.start()
    for slot, copy in enumerate(copies):
        copy.wait()
        out[slot * TBLK : (slot + 1) * TBLK, :] = unit_of(tiles[slot].astype(jnp.float32))


def listed_units(candidates, targets):
    features = targets.shape[1]
    return local_call(
        target_kernel,
        shape((MOST * TBLK, features), jnp.bfloat16),
        (candidates, targets),
        8 * MOST * TBLK * features,
        (
            *SLOTS,
            pltpu.VMEM((MOST, TBLK, features), jnp.bfloat16),
            pltpu.SemaphoreType.DMA((MOST,)),
        ),
        scalars=1,
        place=pl.ANY,
    )


def score_kernel(listed, place, units, *refs):
    parts, (expo, columns, row_total, slots, valid, held) = refs[:-6], refs[-6:]
    find_slots(listed, slots, valid, columns.shape[0])
    gather_refs(parts, held)
    rows = expo.shape[0]
    sort = (place[...] == lax.broadcasted_iota(jnp.int32, (rows, rows), 0)).astype(jnp.bfloat16)
    block = dot(sort, held[...], (1, 0)).astype(jnp.bfloat16)
    scores = dot(block, units[...], (1, 1))
    columns[...] = jnp.zeros_like(columns)
    total = jnp.zeros((rows, 1), jnp.float32)
    for slot in range(MOST):
        part = slice(slot * TBLK, (slot + 1) * TBLK)
        values = jnp.exp(SCORE_SCALE * scores[:, part]) * valid[slot].astype(jnp.float32)
        expo[:, part] = values
        total = total + jnp.sum(values, axis=1, keepdims=True)
        column = jnp.sum(values, axis=0, keepdims=True)

        @pl.when(valid[slot] > 0)
        def _():
            columns[pl.ds(slots[slot], 1), :] = column

    row_total[...] = total


def extra_columns(values):
    lane = lax.broadcasted_iota(jnp.int32, (values[0].shape[0], LANES), 1)
    out = jnp.zeros(lane.shape, jnp.float32)
    for index, value in enumerate(values):
        out = jnp.where(lane == index, value, out)
    return out


def thirds(value):
    first = value.astype(jnp.bfloat16).astype(jnp.float32)
    second = (value - first).astype(jnp.bfloat16).astype(jnp.float32)
    return [first, second, value - first - second]


def match_kernel(listed, expo, columns, row_total, units, own, sent, slots, valid):
    find_slots(listed, slots, valid, columns.shape[0])
    rows = own.shape[0]
    features = units.shape[1]
    mass = jnp.zeros((expo.shape[0], 1), jnp.float32)
    weights = []
    for slot in range(MOST):
        part = pl.ds(slot * TBLK, TBLK)
        values = expo[:, part]
        listed = valid[slot].astype(jnp.float32)
        divisor = jnp.where(listed > 0, columns[pl.ds(slots[slot], 1), :], 1.0)
        mutual = values * (values / divisor)
        mass = mass + jnp.sum(mutual, axis=1, keepdims=True)
        weights.append(mutual.astype(jnp.bfloat16))
    numer = dot(jnp.concatenate(weights, axis=1), units[...], (1, 0))
    totals = row_total[...]
    zero = jnp.zeros((rows, 1), jnp.float32)
    own[:, :features] = numer[:rows]
    own[:, features:] = extra_columns([mass[:rows], zero, zero, totals[:rows]])
    sent[:, :features] = numer[rows:].astype(jnp.bfloat16)
    sent[:, features:] = extra_columns(thirds(mass[rows:]) + thirds(totals[rows:])).astype(
        jnp.bfloat16
    )


def finish_kernel(own, *refs):
    parts, (matched, log_mass) = refs[:-2], refs[-2:]
    rows, features = matched.shape
    total = own[...]
    for part in parts:
        total = total + part[...].astype(jnp.float32)
    numer = total[:, :features]
    square = jnp.mean(numer * numer, axis=-1, keepdims=True)
    matched[...] = (numer * lax.rsqrt(square + 1e-06)).astype(jnp.bfloat16)
    extra = total[:, features:]
    lane = lax.broadcasted_iota(jnp.int32, extra.shape, 1)
    mass = jnp.sum(jnp.where(lane < 3, extra, 0.0), axis=1, keepdims=True)
    whole = jnp.sum(jnp.where(lane < 3, 0.0, extra), axis=1, keepdims=True)
    ratio = mass / whole
    same = lax.broadcasted_iota(jnp.int32, (rows, rows), 0) == lax.broadcasted_iota(
        jnp.int32, (rows, rows), 1
    )
    log_mass[...] = jnp.log(jnp.sum(jnp.where(same, ratio, 0.0), axis=0, keepdims=True))


def far_piece(half):
    held = half
    for axis, bit in [("tgt", b) for b in bits_of("tgt", 2)] + [("src", b) for b in bits_of("src", 4)]:
        held = jnp.concatenate([held, swap(held, axis, bit)])
    return held[half.shape[0] :]


def feed_forward(tokens, inner_weight, outer_weight):
    barrier = lax.optimization_barrier
    inner_x, outer_x = swap(inner_weight, "src", 2), swap(outer_weight, "src", 2)
    inner_half, outer_half = weight_halves(inner_weight, outer_weight)
    inner_far, outer_far = far_piece(inner_half), far_piece(outer_half)
    neighbour = swap(tokens, "tgt", 1)
    inner_far_x, inner_far_y = swap(inner_far, "src", 2), swap(inner_far, "groups", 1)

    outer_far, inner_far_y, outer_x, inner_x = barrier((outer_far, inner_far_y, outer_x, inner_x))
    outer_far_x, outer_far_y = swap(outer_far, "src", 2), swap(outer_far, "groups", 1)
    inner_square = [inner_far_x, inner_far_y, swap(inner_far_y, "src", 2)]
    outer_square = [outer_far_x, outer_far_y, swap(outer_far_x, "groups", 1)]
    shared = [tokens, neighbour, swap(tokens, "src", 1), swap(neighbour, "src", 1)]
    hidden = [
        hidden_units(shared, [inner_weight, inner_x]),
        hidden_units(shared, [inner_far, *inner_square]),
    ]

    weights = [outer_weight, outer_x, outer_far, *outer_square]
    pair, own = partial_sums(hidden, weights, (3, 2))
    pair, own = swap(pair, "src", 1), swap(own, "src", 1)
    (back,) = partial_sums(hidden, weights, (1,), (pair,))
    back, hidden = barrier((back, hidden))
    back = swap(back, "tgt", 1)
    (own,) = partial_sums(hidden, weights, (0,), (tokens, own), jnp.float32)
    return own, back


def on_device(tokens, sentence_ids, inner_weight, outer_weight, grid_rows, candidates, targets):
    features = tokens.shape[1]
    src_count = lax.axis_size("src")
    tgt_count = lax.axis_size("tgt")
    src_index = lax.axis_index("src")
    tgt_index = lax.axis_index("tgt")
    per_block = SENT_DEV // src_count
    block_rows = tgt_count * SENT_DEV

    column_blocks = targets.shape[0] // TBLK
    target_units = listed_units(candidates, targets)

    summands = feed_forward(tokens, inner_weight, outer_weight)
    order_key = (grid_rows // block_rows ^ src_index) * per_block + grid_rows % per_block
    held = local_call(
        pool_kernel,
        shape((SENT_DEV, features), jnp.bfloat16),
        (sentence_ids, order_key.reshape(1, -1), *summands),
        20 * tokens.shape[0] * features,
    )
    held = held.reshape(src_count, 1, per_block, features)
    for bit in reversed(bits_of("src", 1)):
        held = jnp.concatenate([held[:bit], swap(held[bit:], "src", bit)], axis=1)
    mine = held.reshape(SENT_DEV, features)
    parts = [mine] + [swap(mine, "tgt", offset) for offset in range(1, tgt_count)]
    origin = jnp.arange(1, dtype=jnp.int32)
    for bit in reversed(bits_of("src", 1)):
        origin = jnp.concatenate([origin, origin ^ bit])
    from_src = (origin ^ src_index)[None, :, None]
    from_tgt = (jnp.arange(tgt_count, dtype=jnp.int32) ^ tgt_index)[:, None, None]
    place = (from_src * tgt_count + from_tgt) * per_block + jnp.arange(per_block, dtype=jnp.int32)
    place = place.reshape(1, -1) ^ (tgt_index * SENT_DEV)

    pairs = MOST * TBLK
    expo, column_total, row_total = local_call(
        score_kernel,
        (
            shape((block_rows, pairs), jnp.float32),
            shape((column_blocks, TBLK), jnp.float32),
            shape((block_rows, 1), jnp.float32),
        ),
        (candidates, place, target_units, *parts),
        2 * block_rows * pairs * features,
        (*SLOTS, pltpu.VMEM((block_rows, features), jnp.bfloat16)),
        scalars=1,
    )
    for bit in bits_of("src", 1):
        column_total = column_total + swap(column_total, "src", bit)
    own, sent = local_call(
        match_kernel,
        (
            shape((SENT_DEV, features + LANES), jnp.float32),
            shape((block_rows - SENT_DEV, features + LANES), jnp.bfloat16),
        ),
        (candidates, expo, column_total, row_total, target_units),
        2 * block_rows * pairs * features,
        SLOTS,
        scalars=1,
    )
    received = [
        swap(sent[(offset - 1) * SENT_DEV : offset * SENT_DEV], "tgt", offset)
        for offset in range(1, tgt_count)
    ]
    matched, log_mass = local_call(
        finish_kernel,
        (shape((SENT_DEV, features), jnp.bfloat16), shape((1, SENT_DEV), jnp.float32)),
        (own, *received),
        8 * SENT_DEV * features,
    )
    return (matched, log_mass.reshape(SENT_DEV))


def solution(mesh):
    in_specs = (
        P(("groups", "src", "tgt"), None),
        P(("groups", "src", "tgt"), None),
        P(("src", "tgt"), None),
        P(("src", "tgt"), None),
        P(("groups", "src", "tgt")),
        P(("groups", "src"), None),
        P(("groups", "tgt"), None),
    )
    out_specs = (P(("groups", "src", "tgt"), None), P(("groups", "src", "tgt")))
    return jax.shard_map(
        on_device, mesh=mesh, in_specs=in_specs, out_specs=out_specs, check_vma=False
    )
```

```python
import functools
import math

import jax
import jax.numpy as jnp
from jax import lax
from jax.experimental import pallas as pl
from jax.experimental.pallas import tpu as pltpu
from jax.sharding import PartitionSpec as P

SENT_DEV = 32
TBLK = 256
MOST = 4
LANES = 128


SCORE_SCALE = 32.0


def bits_of(axis, first):
    size, bit, bits = lax.axis_size(axis), first, []
    while bit < size:
        bits.append(bit)
        bit *= 2
    return bits


def swap(values, axis, offset):
    return lax.ppermute(values, axis, [(i, i ^ offset) for i in range(lax.axis_size(axis))])


def local_call(
    kernel, out_shape, args, flops, scratch=(), scalars=0, near=0, place=pltpu.VMEM, vmem=16
):
    outs = out_shape if isinstance(out_shape, tuple) else (out_shape,)
    moved = sum(math.prod(a.shape) * a.dtype.itemsize for a in (*args, *outs))
    return pl.pallas_call(
        kernel,
        out_shape=out_shape,
        in_specs=[pl.BlockSpec(memory_space=pltpu.SMEM)] * scalars
        + [pl.BlockSpec(memory_space=pltpu.VMEM)] * near
        + [pl.BlockSpec(memory_space=place)] * (len(args) - scalars - near),
        out_specs=jax.tree.map(lambda _: pl.BlockSpec(memory_space=pltpu.VMEM), out_shape),
        scratch_shapes=scratch,
        compiler_params=pltpu.CompilerParams(vmem_limit_bytes=vmem * 2**20),
        cost_estimate=pl.CostEstimate(flops=flops, bytes_accessed=moved, transcendentals=0),
    )(*args)


def shape(dims, dtype):
    return jax.ShapeDtypeStruct(tuple(dims), dtype)


def unit_of(floats):
    square = jnp.mean(floats * floats, axis=-1, keepdims=True)
    return (floats * lax.rsqrt(square + 1e-06) * (1.0 / math.sqrt(floats.shape[-1]))).astype(
        jnp.bfloat16
    )


def dot(left, right, contract, **more):
    return lax.dot_general(
        left, right, ((contract[:1], contract[1:]), ((), ())),
        preferred_element_type=jnp.float32, **more
    )


def gather_refs(refs, held):
    start = 0
    for ref in refs:
        held[start : start + ref.shape[0], :] = ref[...]
        start += ref.shape[0]


def fetches(refs, held, sems):
    start, copies = 0, []
    for index, ref in enumerate(refs):
        count = ref.shape[0]
        copies.append(
            pltpu.make_async_copy(ref, held.at[pl.ds(start, count)], sems.at[index])
        )
        start += count
    for copy in copies:
        copy.start()
    return copies


def slice_kernel(inner, outer, inner_half, outer_half, sems):
    half = inner_half.shape[0]
    rows = pl.ds(pl.multiple_of(lax.axis_index("groups") * half, half), half)
    copies = [
        pltpu.make_async_copy(inner.at[rows], inner_half, sems.at[0]),
        pltpu.make_async_copy(outer.at[rows], outer_half, sems.at[1]),
    ]
    for copy in copies:
        copy.start()
    for copy in copies:
        copy.wait()


def weight_halves(inner, outer):
    units, features = inner.shape
    return local_call(
        slice_kernel,
        (shape((units // 2, features), jnp.bfloat16),) * 2,
        (inner, outer),
        0,
        (pltpu.SemaphoreType.DMA((2,)),),
        place=pl.ANY,
        vmem=58,
    )


def hidden_kernel(count, *refs):
    tokens, weights, (out, held, sems) = refs[:count], refs[count:-3], refs[-3:]
    for copy in fetches(weights, held, sems):
        copy.wait()
    start = 0
    for token in tokens:
        part = pl.ds(start, token.shape[0])
        product = dot(token[...], held[...], (1, 1))
        out[part, :] = (
            product * 0.5 * (1.0 + lax.erf(product * math.sqrt(0.5)))
        ).astype(jnp.bfloat16)
        start += token.shape[0]


def hidden_units(tokens, weights):
    features = weights[0].shape[1]
    rows = sum(t.shape[0] for t in tokens)
    units = sum(w.shape[0] for w in weights)
    return local_call(
        functools.partial(hidden_kernel, len(tokens)),
        shape((rows, units), jnp.bfloat16),
        (*tokens, *weights),
        2 * rows * units * features,
        (
            pltpu.VMEM((units, features), jnp.bfloat16),
            pltpu.SemaphoreType.DMA((len(weights),)),
        ),
        near=len(tokens),
        place=pl.ANY,
    )


def partial_kernel(blocks, added, near, far, *refs):
    terms, refs = refs[:added], refs[added:]
    split = near.shape[1]
    weights, outs, (held, sems) = refs[: -len(blocks) - 2], refs[-len(blocks) - 2 : -2], refs[-2:]
    for copy in fetches(weights, held, sems):
        copy.wait()
    for index, out in zip(blocks, outs):
        rows = out.shape[0]
        part = pl.ds(index * rows, rows)
        sums = dot(near[part, :], held[:split, :], (1, 0)) + dot(far[part, :], held[split:, :], (1, 0))
        for term in terms:
            sums = sums + term[...].astype(jnp.float32)
        out[...] = sums.astype(out.dtype)


def partial_sums(hidden, weights, blocks, terms=(), dtype=jnp.bfloat16):
    rows, features = hidden[0].shape[0] // 4, weights[0].shape[1]
    units = hidden[0].shape[1] + hidden[1].shape[1]
    return local_call(
        functools.partial(partial_kernel, blocks, len(terms)),
        (shape((rows, features), dtype),) * len(blocks),
        (*hidden, *terms, *weights),
        2 * len(blocks) * rows * units * features,
        (
            pltpu.VMEM((units, features), jnp.bfloat16),
            pltpu.SemaphoreType.DMA((len(weights),)),
        ),
        near=2 + len(terms),
        place=pl.ANY,
    )


def pool_kernel(identity, order, own, back, out):
    summed = own[...] + back[...].astype(jnp.float32)
    center = jnp.mean(summed, axis=-1, keepdims=True)
    moved = summed - center
    spread = jnp.mean(moved * moved, axis=-1, keepdims=True)
    normed = moved * lax.rsqrt(spread + 1e-05)
    sentences = out.shape[0]
    members = (
        identity[...] == lax.broadcasted_iota(jnp.int32, (sentences, own.shape[0]), 0)
    ).astype(jnp.float32)
    sums = dot(members, normed, (1, 0), precision=lax.Precision.HIGHEST)
    unit = unit_of(sums / jnp.sum(members, axis=1, keepdims=True))
    sort = (order[...] == lax.broadcasted_iota(jnp.int32, (sentences, sentences), 0)).astype(
        jnp.bfloat16
    )
    out[...] = dot(sort, unit, (1, 0)).astype(jnp.bfloat16)


def find_slots(listed, slots, valid, blocks):
    column = lax.axis_index("tgt")
    for slot in range(MOST):
        slots[slot] = 0
        valid[slot] = 0
    count = jnp.int32(0)
    for index in range(listed.shape[1]):
        block = listed[0, index]
        here = lax.div(block, blocks) == column

        @pl.when(here)
        def _():
            slots[count] = lax.rem(block, blocks)
            valid[count] = 1

        count = count + here.astype(jnp.int32)


SLOTS = (pltpu.SMEM((MOST,), jnp.int32),) * 2


def target_kernel(listed, targets, out, slots, valid, tiles, sems):
    find_slots(listed, slots, valid, targets.shape[0] // TBLK)
    copies = [
        pltpu.make_async_copy(
            targets.at[pl.ds(pl.multiple_of(slots[slot] * TBLK, TBLK), TBLK)],
            tiles.at[slot],
            sems.at[slot],
        )
        for slot in range(MOST)
    ]
    for copy in copies:
        copy.start()
    for slot, copy in enumerate(copies):
        copy.wait()
        out[slot * TBLK : (slot + 1) * TBLK, :] = unit_of(tiles[slot].astype(jnp.float32))


def listed_units(candidates, targets):
    features = targets.shape[1]
    return local_call(
        target_kernel,
        shape((MOST * TBLK, features), jnp.bfloat16),
        (candidates, targets),
        8 * MOST * TBLK * features,
        (
            *SLOTS,
            pltpu.VMEM((MOST, TBLK, features), jnp.bfloat16),
            pltpu.SemaphoreType.DMA((MOST,)),
        ),
        scalars=1,
        place=pl.ANY,
    )


def score_kernel(listed, place, units, *refs):
    parts, (expo, columns, row_total, slots, valid, held) = refs[:-6], refs[-6:]
    find_slots(listed, slots, valid, columns.shape[0])
    gather_refs(parts, held)
    rows = expo.shape[0]
    sort = (place[...] == lax.broadcasted_iota(jnp.int32, (rows, rows), 0)).astype(jnp.bfloat16)
    block = dot(sort, held[...], (1, 0)).astype(jnp.bfloat16)
    scores = dot(block, units[...], (1, 1))
    columns[...] = jnp.zeros_like(columns)
    total = jnp.zeros((rows, 1), jnp.float32)
    for slot in range(MOST):
        part = slice(slot * TBLK, (slot + 1) * TBLK)
        values = jnp.exp(SCORE_SCALE * scores[:, part]) * valid[slot].astype(jnp.float32)
        expo[:, part] = values
        total = total + jnp.sum(values, axis=1, keepdims=True)
        column = jnp.sum(values, axis=0, keepdims=True)

        @pl.when(valid[slot] > 0)
        def _():
            columns[pl.ds(slots[slot], 1), :] = column

    row_total[...] = total


def extra_columns(values):
    lane = lax.broadcasted_iota(jnp.int32, (values[0].shape[0], LANES), 1)
    out = jnp.zeros(lane.shape, jnp.float32)
    for index, value in enumerate(values):
        out = jnp.where(lane == index, value, out)
    return out


def thirds(value):
    first = value.astype(jnp.bfloat16).astype(jnp.float32)
    second = (value - first).astype(jnp.bfloat16).astype(jnp.float32)
    return [first, second, value - first - second]


def match_kernel(listed, expo, columns, row_total, units, own, sent, slots, valid):
    find_slots(listed, slots, valid, columns.shape[0])
    rows = own.shape[0]
    features = units.shape[1]
    mass = jnp.zeros((expo.shape[0], 1), jnp.float32)
    weights = []
    for slot in range(MOST):
        part = pl.ds(slot * TBLK, TBLK)
        values = expo[:, part]
        listed = valid[slot].astype(jnp.float32)
        divisor = jnp.where(listed > 0, columns[pl.ds(slots[slot], 1), :], 1.0)
        mutual = values * (values / divisor)
        mass = mass + jnp.sum(mutual, axis=1, keepdims=True)
        weights.append(mutual.astype(jnp.bfloat16))
    numer = dot(jnp.concatenate(weights, axis=1), units[...], (1, 0))
    totals = row_total[...]
    zero = jnp.zeros((rows, 1), jnp.float32)
    own[:, :features] = numer[:rows]
    own[:, features:] = extra_columns([mass[:rows], zero, zero, totals[:rows]])
    sent[:, :features] = numer[rows:].astype(jnp.bfloat16)
    sent[:, features:] = extra_columns(thirds(mass[rows:]) + thirds(totals[rows:])).astype(
        jnp.bfloat16
    )


def finish_kernel(own, *refs):
    parts, (matched, log_mass) = refs[:-2], refs[-2:]
    rows, features = matched.shape
    total = own[...]
    for part in parts:
        total = total + part[...].astype(jnp.float32)
    numer = total[:, :features]
    square = jnp.mean(numer * numer, axis=-1, keepdims=True)
    matched[...] = (numer * lax.rsqrt(square + 1e-06)).astype(jnp.bfloat16)
    extra = total[:, features:]
    lane = lax.broadcasted_iota(jnp.int32, extra.shape, 1)
    mass = jnp.sum(jnp.where(lane < 3, extra, 0.0), axis=1, keepdims=True)
    whole = jnp.sum(jnp.where(lane < 3, 0.0, extra), axis=1, keepdims=True)
    ratio = mass / whole
    same = lax.broadcasted_iota(jnp.int32, (rows, rows), 0) == lax.broadcasted_iota(
        jnp.int32, (rows, rows), 1
    )
    log_mass[...] = jnp.log(jnp.sum(jnp.where(same, ratio, 0.0), axis=0, keepdims=True))


def far_piece(half):
    held = half
    for axis, bit in [("tgt", b) for b in bits_of("tgt", 2)] + [("src", b) for b in bits_of("src", 4)]:
        held = jnp.concatenate([held, swap(held, axis, bit)])
    return held[half.shape[0] :]


def feed_forward(tokens, inner_weight, outer_weight):
    barrier = lax.optimization_barrier
    inner_x, outer_x = swap(inner_weight, "src", 2), swap(outer_weight, "src", 2)
    inner_half, outer_half = weight_halves(inner_weight, outer_weight)
    inner_far, outer_far = far_piece(inner_half), far_piece(outer_half)
    neighbour = swap(tokens, "tgt", 1)
    inner_far_x, inner_far_y = swap(inner_far, "src", 2), swap(inner_far, "groups", 1)

    outer_far, inner_far_y, outer_x, inner_x = barrier((outer_far, inner_far_y, outer_x, inner_x))
    outer_far_x, outer_far_y = swap(outer_far, "src", 2), swap(outer_far, "groups", 1)
    inner_square = [inner_far_x, inner_far_y, swap(inner_far_y, "src", 2)]
    outer_square = [outer_far_x, outer_far_y, swap(outer_far_x, "groups", 1)]
    shared = [tokens, neighbour, swap(tokens, "src", 1), swap(neighbour, "src", 1)]
    hidden = [
        hidden_units(shared, [inner_weight, inner_x]),
        hidden_units(shared, [inner_far, *inner_square]),
    ]

    weights = [outer_weight, outer_x, outer_far, *outer_square]
    (pair,) = partial_sums(hidden, weights, (3,))
    hidden, pair = barrier((hidden, pair))
    (core,) = partial_sums(hidden, weights, (2,))
    pair, core = barrier((swap(pair, "src", 1), core))
    (back,) = partial_sums(hidden, weights, (1,), (pair,))
    back, core, hidden = barrier((back, core, hidden))
    back = swap(back, "tgt", 1)
    (own,) = partial_sums(hidden, weights, (0,), (tokens, swap(core, "src", 1)), jnp.float32)
    return own, back


def on_device(tokens, sentence_ids, inner_weight, outer_weight, grid_rows, candidates, targets):
    features = tokens.shape[1]
    src_count = lax.axis_size("src")
    tgt_count = lax.axis_size("tgt")
    src_index = lax.axis_index("src")
    tgt_index = lax.axis_index("tgt")
    per_block = SENT_DEV // src_count
    block_rows = tgt_count * SENT_DEV

    column_blocks = targets.shape[0] // TBLK
    target_units = listed_units(candidates, targets)

    summands = feed_forward(tokens, inner_weight, outer_weight)
    order_key = (grid_rows // block_rows ^ src_index) * per_block + grid_rows % per_block
    held = local_call(
        pool_kernel,
        shape((SENT_DEV, features), jnp.bfloat16),
        (sentence_ids, order_key.reshape(1, -1), *summands),
        20 * tokens.shape[0] * features,
    )
    held = held.reshape(src_count, 1, per_block, features)
    for bit in reversed(bits_of("src", 1)):
        held = jnp.concatenate([held[:bit], swap(held[bit:], "src", bit)], axis=1)
    mine = held.reshape(SENT_DEV, features)
    parts = [mine] + [swap(mine, "tgt", offset) for offset in range(1, tgt_count)]
    origin = jnp.arange(1, dtype=jnp.int32)
    for bit in reversed(bits_of("src", 1)):
        origin = jnp.concatenate([origin, origin ^ bit])
    from_src = (origin ^ src_index)[None, :, None]
    from_tgt = (jnp.arange(tgt_count, dtype=jnp.int32) ^ tgt_index)[:, None, None]
    place = (from_src * tgt_count + from_tgt) * per_block + jnp.arange(per_block, dtype=jnp.int32)
    place = place.reshape(1, -1) ^ (tgt_index * SENT_DEV)

    pairs = MOST * TBLK
    expo, column_total, row_total = local_call(
        score_kernel,
        (
            shape((block_rows, pairs), jnp.float32),
            shape((column_blocks, TBLK), jnp.float32),
            shape((block_rows, 1), jnp.float32),
        ),
        (candidates, place, target_units, *parts),
        2 * block_rows * pairs * features,
        (*SLOTS, pltpu.VMEM((block_rows, features), jnp.bfloat16)),
        scalars=1,
    )
    for bit in bits_of("src", 1):
        column_total = column_total + swap(column_total, "src", bit)
    own, sent = local_call(
        match_kernel,
        (
            shape((SENT_DEV, features + LANES), jnp.float32),
            shape((block_rows - SENT_DEV, features + LANES), jnp.bfloat16),
        ),
        (candidates, expo, column_total, row_total, target_units),
        2 * block_rows * pairs * features,
        SLOTS,
        scalars=1,
    )
    received = [
        swap(sent[(offset - 1) * SENT_DEV : offset * SENT_DEV], "tgt", offset)
        for offset in range(1, tgt_count)
    ]
    matched, log_mass = local_call(
        finish_kernel,
        (shape((SENT_DEV, features), jnp.bfloat16), shape((1, SENT_DEV), jnp.float32)),
        (own, *received),
        8 * SENT_DEV * features,
    )
    return (matched, log_mass.reshape(SENT_DEV))


def solution(mesh):
    in_specs = (
        P(("groups", "src", "tgt"), None),
        P(("groups", "src", "tgt"), None),
        P(("src", "tgt"), None),
        P(("src", "tgt"), None),
        P(("groups", "src", "tgt")),
        P(("groups", "src"), None),
        P(("groups", "tgt"), None),
    )
    out_specs = (P(("groups", "src", "tgt"), None), P(("groups", "src", "tgt")))
    return jax.shard_map(
        on_device, mesh=mesh, in_specs=in_specs, out_specs=out_specs, check_vma=False
    )
```

```python
import functools
import math

import jax
import jax.numpy as jnp
from jax import lax
from jax.experimental import pallas as pl
from jax.experimental.pallas import tpu as pltpu
from jax.sharding import PartitionSpec as P

SENT_DEV = 32
TBLK = 256
MOST = 4
LANES = 128


SCORE_SCALE = 32.0


def bits_of(axis, first):
    size, bit, bits = lax.axis_size(axis), first, []
    while bit < size:
        bits.append(bit)
        bit *= 2
    return bits


def swap(values, axis, offset):
    return lax.ppermute(values, axis, [(i, i ^ offset) for i in range(lax.axis_size(axis))])


def local_call(
    kernel, out_shape, args, flops, scratch=(), scalars=0, near=0, place=pltpu.VMEM, vmem=16
):
    outs = out_shape if isinstance(out_shape, tuple) else (out_shape,)
    moved = sum(math.prod(a.shape) * a.dtype.itemsize for a in (*args, *outs))
    return pl.pallas_call(
        kernel,
        out_shape=out_shape,
        in_specs=[pl.BlockSpec(memory_space=pltpu.SMEM)] * scalars
        + [pl.BlockSpec(memory_space=pltpu.VMEM)] * near
        + [pl.BlockSpec(memory_space=place)] * (len(args) - scalars - near),
        out_specs=jax.tree.map(lambda _: pl.BlockSpec(memory_space=pltpu.VMEM), out_shape),
        scratch_shapes=scratch,
        compiler_params=pltpu.CompilerParams(vmem_limit_bytes=vmem * 2**20),
        cost_estimate=pl.CostEstimate(flops=flops, bytes_accessed=moved, transcendentals=0),
    )(*args)


def shape(dims, dtype):
    return jax.ShapeDtypeStruct(tuple(dims), dtype)


def unit_of(floats):
    square = jnp.mean(floats * floats, axis=-1, keepdims=True)
    return (floats * lax.rsqrt(square + 1e-06) * (1.0 / math.sqrt(floats.shape[-1]))).astype(
        jnp.bfloat16
    )


def dot(left, right, contract, **more):
    return lax.dot_general(
        left, right, ((contract[:1], contract[1:]), ((), ())),
        preferred_element_type=jnp.float32, **more
    )


def gather_refs(refs, held):
    start = 0
    for ref in refs:
        held[start : start + ref.shape[0], :] = ref[...]
        start += ref.shape[0]


def fetches(refs, held, sems, paired=None):
    start, copies = 0, []
    for index, ref in enumerate(refs):
        count = ref.shape[0]
        place = start
        if paired is not None and index in (paired, paired + 1):
            first = lax.axis_index("groups")
            step = first if index == paired else -first
            place = pl.multiple_of(start + step * count, count)
        copies.append(
            pltpu.make_async_copy(ref, held.at[pl.ds(place, count)], sems.at[index])
        )
        start += count
    for copy in copies:
        copy.start()
    return copies


def slice_kernel(inner, outer, inner_half, outer_half, sems):
    half = inner_half.shape[0]
    rows = pl.ds(pl.multiple_of(lax.axis_index("groups") * half, half), half)
    copies = [
        pltpu.make_async_copy(inner.at[rows], inner_half, sems.at[0]),
        pltpu.make_async_copy(outer.at[rows], outer_half, sems.at[1]),
    ]
    for copy in copies:
        copy.start()
    for copy in copies:
        copy.wait()


def weight_halves(inner, outer):
    units, features = inner.shape
    return local_call(
        slice_kernel,
        (shape((units // 2, features), jnp.bfloat16),) * 2,
        (inner, outer),
        0,
        (pltpu.SemaphoreType.DMA((2,)),),
        place=pl.ANY,
        vmem=58,
    )


def hidden_kernel(count, *refs):
    tokens, weights, (out, held, sems) = refs[:count], refs[count:-3], refs[-3:]
    for copy in fetches(weights, held, sems):
        copy.wait()
    start = 0
    for token in tokens:
        part = pl.ds(start, token.shape[0])
        product = dot(token[...], held[...], (1, 1))
        out[part, :] = (
            product * 0.5 * (1.0 + lax.erf(product * math.sqrt(0.5)))
        ).astype(jnp.bfloat16)
        start += token.shape[0]


def hidden_units(tokens, weights):
    features = weights[0].shape[1]
    rows = sum(t.shape[0] for t in tokens)
    units = sum(w.shape[0] for w in weights)
    return local_call(
        functools.partial(hidden_kernel, len(tokens)),
        shape((rows, units), jnp.bfloat16),
        (*tokens, *weights),
        2 * rows * units * features,
        (
            pltpu.VMEM((units, features), jnp.bfloat16),
            pltpu.SemaphoreType.DMA((len(weights),)),
        ),
        near=len(tokens),
        place=pl.ANY,
    )


def partial_kernel(blocks, added, near, far, *refs):
    terms, refs = refs[:added], refs[added:]
    split = near.shape[1]
    weights, outs, (held, sems) = refs[: -len(blocks) - 2], refs[-len(blocks) - 2 : -2], refs[-2:]
    for copy in fetches(weights, held, sems, paired=1):
        copy.wait()
    for index, out in zip(blocks, outs):
        rows = out.shape[0]
        part = pl.ds(index * rows, rows)
        sums = dot(near[part, :], held[:split, :], (1, 0)) + dot(far[part, :], held[split:, :], (1, 0))
        for term in terms:
            sums = sums + term[...].astype(jnp.float32)
        out[...] = sums.astype(out.dtype)


def return_kernel(near, far, core, *refs):
    weights, (first, second, held, sems) = refs[:-4], refs[-4:]
    for copy in fetches(weights, held, sems, paired=1):
        copy.wait()
    rows, split = first.shape[0], near.shape[1]
    for index, out in enumerate((first, second)):
        part = pl.ds((2 + index) * rows, rows)
        sums = dot(near[part, :], held[:split, :], (1, 0)) + dot(far[part, :], held[split:, :], (1, 0))
        out[...] = (sums + core[index * rows : (index + 1) * rows, :].astype(jnp.float32)).astype(
            out.dtype
        )


def return_sums(hidden, weights, core):
    rows, features = core.shape
    units = hidden[0].shape[1] + hidden[1].shape[1]
    return local_call(
        return_kernel,
        (shape((rows // 2, features), jnp.bfloat16),) * 2,
        (*hidden, core, *weights),
        2 * rows * units * features,
        (
            pltpu.VMEM((units, features), jnp.bfloat16),
            pltpu.SemaphoreType.DMA((len(weights),)),
        ),
        near=3,
        place=pl.ANY,
    )


def partial_sums(hidden, weights, blocks, terms=(), dtype=jnp.bfloat16):
    rows, features = hidden[0].shape[0] // 4, weights[0].shape[1]
    units = hidden[0].shape[1] + hidden[1].shape[1]
    return local_call(
        functools.partial(partial_kernel, blocks, len(terms)),
        (shape((rows, features), dtype),) * len(blocks),
        (*hidden, *terms, *weights),
        2 * len(blocks) * rows * units * features,
        (
            pltpu.VMEM((units, features), jnp.bfloat16),
            pltpu.SemaphoreType.DMA((len(weights),)),
        ),
        near=2 + len(terms),
        place=pl.ANY,
    )


def pool_kernel(identity, order, own, first, second, out):
    summed = own[...] + jnp.concatenate([first[...], second[...]], axis=0).astype(jnp.float32)
    center = jnp.mean(summed, axis=-1, keepdims=True)
    moved = summed - center
    spread = jnp.mean(moved * moved, axis=-1, keepdims=True)
    normed = moved * lax.rsqrt(spread + 1e-05)
    sentences = out.shape[0]
    members = (
        identity[...] == lax.broadcasted_iota(jnp.int32, (sentences, own.shape[0]), 0)
    ).astype(jnp.float32)
    sums = dot(members, normed, (1, 0), precision=lax.Precision.HIGHEST)
    unit = unit_of(sums / jnp.sum(members, axis=1, keepdims=True))
    sort = (order[...] == lax.broadcasted_iota(jnp.int32, (sentences, sentences), 0)).astype(
        jnp.bfloat16
    )
    out[...] = dot(sort, unit, (1, 0)).astype(jnp.bfloat16)


def find_slots(listed, slots, valid, blocks):
    column = lax.axis_index("tgt")
    for slot in range(MOST):
        slots[slot] = 0
        valid[slot] = 0
    count = jnp.int32(0)
    for index in range(listed.shape[1]):
        block = listed[0, index]
        here = lax.div(block, blocks) == column

        @pl.when(here)
        def _():
            slots[count] = lax.rem(block, blocks)
            valid[count] = 1

        count = count + here.astype(jnp.int32)


SLOTS = (pltpu.SMEM((MOST,), jnp.int32),) * 2


def target_kernel(listed, targets, out, slots, valid, tiles, sems):
    find_slots(listed, slots, valid, targets.shape[0] // TBLK)
    copies = [
        pltpu.make_async_copy(
            targets.at[pl.ds(pl.multiple_of(slots[slot] * TBLK, TBLK), TBLK)],
            tiles.at[slot],
            sems.at[slot],
        )
        for slot in range(MOST)
    ]
    for copy in copies:
        copy.start()
    for slot, copy in enumerate(copies):
        copy.wait()
        out[slot * TBLK : (slot + 1) * TBLK, :] = unit_of(tiles[slot].astype(jnp.float32))


def listed_units(candidates, targets):
    features = targets.shape[1]
    return local_call(
        target_kernel,
        shape((MOST * TBLK, features), jnp.bfloat16),
        (candidates, targets),
        8 * MOST * TBLK * features,
        (
            *SLOTS,
            pltpu.VMEM((MOST, TBLK, features), jnp.bfloat16),
            pltpu.SemaphoreType.DMA((MOST,)),
        ),
        scalars=1,
        place=pl.ANY,
    )


def score_kernel(listed, place, units, *refs):
    parts, (expo, columns, row_total, slots, valid, held) = refs[:-6], refs[-6:]
    find_slots(listed, slots, valid, columns.shape[0])
    gather_refs(parts, held)
    rows = expo.shape[0]
    sort = (place[...] == lax.broadcasted_iota(jnp.int32, (rows, rows), 0)).astype(jnp.bfloat16)
    block = dot(sort, held[...], (1, 0)).astype(jnp.bfloat16)
    scores = dot(block, units[...], (1, 1))
    columns[...] = jnp.zeros_like(columns)
    total = jnp.zeros((rows, 1), jnp.float32)
    for slot in range(MOST):
        part = slice(slot * TBLK, (slot + 1) * TBLK)
        values = jnp.exp(SCORE_SCALE * scores[:, part]) * valid[slot].astype(jnp.float32)
        expo[:, part] = values
        total = total + jnp.sum(values, axis=1, keepdims=True)
        column = jnp.sum(values, axis=0, keepdims=True)

        @pl.when(valid[slot] > 0)
        def _():
            columns[pl.ds(slots[slot], 1), :] = column

    row_total[...] = total


def extra_columns(values):
    lane = lax.broadcasted_iota(jnp.int32, (values[0].shape[0], LANES), 1)
    out = jnp.zeros(lane.shape, jnp.float32)
    for index, value in enumerate(values):
        out = jnp.where(lane == index, value, out)
    return out


def thirds(value):
    first = value.astype(jnp.bfloat16).astype(jnp.float32)
    second = (value - first).astype(jnp.bfloat16).astype(jnp.float32)
    return [first, second, value - first - second]


def match_kernel(listed, expo, columns, row_total, units, own, sent, slots, valid):
    find_slots(listed, slots, valid, columns.shape[0])
    rows = own.shape[0]
    features = units.shape[1]
    mass = jnp.zeros((expo.shape[0], 1), jnp.float32)
    weights = []
    for slot in range(MOST):
        part = pl.ds(slot * TBLK, TBLK)
        values = expo[:, part]
        listed = valid[slot].astype(jnp.float32)
        divisor = jnp.where(listed > 0, columns[pl.ds(slots[slot], 1), :], 1.0)
        mutual = values * (values / divisor)
        mass = mass + jnp.sum(mutual, axis=1, keepdims=True)
        weights.append(mutual.astype(jnp.bfloat16))
    numer = dot(jnp.concatenate(weights, axis=1), units[...], (1, 0))
    totals = row_total[...]
    zero = jnp.zeros((rows, 1), jnp.float32)
    own[:, :features] = numer[:rows]
    own[:, features:] = extra_columns([mass[:rows], zero, zero, totals[:rows]])
    sent[:, :features] = numer[rows:].astype(jnp.bfloat16)
    sent[:, features:] = extra_columns(thirds(mass[rows:]) + thirds(totals[rows:])).astype(
        jnp.bfloat16
    )


def finish_kernel(own, *refs):
    parts, (matched, log_mass) = refs[:-2], refs[-2:]
    rows, features = matched.shape
    total = own[...]
    for part in parts:
        total = total + part[...].astype(jnp.float32)
    numer = total[:, :features]
    square = jnp.mean(numer * numer, axis=-1, keepdims=True)
    matched[...] = (numer * lax.rsqrt(square + 1e-06)).astype(jnp.bfloat16)
    extra = total[:, features:]
    lane = lax.broadcasted_iota(jnp.int32, extra.shape, 1)
    mass = jnp.sum(jnp.where(lane < 3, extra, 0.0), axis=1, keepdims=True)
    whole = jnp.sum(jnp.where(lane < 3, 0.0, extra), axis=1, keepdims=True)
    ratio = mass / whole
    same = lax.broadcasted_iota(jnp.int32, (rows, rows), 0) == lax.broadcasted_iota(
        jnp.int32, (rows, rows), 1
    )
    log_mass[...] = jnp.log(jnp.sum(jnp.where(same, ratio, 0.0), axis=0, keepdims=True))


def far_piece(half):
    held = half
    for axis, bit in [("tgt", b) for b in bits_of("tgt", 2)] + [("src", b) for b in bits_of("src", 4)]:
        held = jnp.concatenate([held, swap(held, axis, bit)])
    return held[half.shape[0] :]


def feed_forward(tokens, inner_weight, outer_weight):
    barrier = lax.optimization_barrier
    inner_half, outer_half = weight_halves(inner_weight, outer_weight)
    inner_x, outer_x = swap(inner_weight, "src", 2), swap(outer_half, "src", 2)
    inner_far, outer_far = far_piece(inner_half), far_piece(outer_half)
    neighbour = swap(tokens, "tgt", 1)
    inner_far_x = swap(inner_far, "src", 2)

    outer_y = swap(outer_x, "groups", 1)
    inner_far, outer_far, inner_far_x, outer_y, inner_x = barrier(
        (inner_far, outer_far, inner_far_x, outer_y, inner_x)
    )
    inner_far_y = swap(inner_far, "groups", 1)
    outer_far_x, outer_far_y = swap(outer_far, "src", 2), swap(outer_far, "groups", 1)
    inner_square = [inner_far_x, inner_far_y, swap(inner_far_y, "src", 2)]
    outer_square = [outer_far_x, outer_far_y, swap(outer_far_x, "groups", 1)]
    shared = [tokens, neighbour, swap(tokens, "src", 1), swap(neighbour, "src", 1)]
    inner_square[2], outer_square[1] = barrier((inner_square[2], outer_square[1]))
    hidden = [
        hidden_units(shared, [inner_weight, inner_x, inner_far, inner_square[0]]),
        hidden_units(shared, inner_square[1:]),
    ]

    weights = [outer_weight, outer_x, outer_y, outer_far, *outer_square]
    (pair,) = partial_sums(hidden, weights, (3,))
    hidden, pair = barrier((hidden, pair))
    (core,) = partial_sums(hidden, weights, (2,))
    pair, core = barrier((swap(pair, "src", 1), core))
    back = return_sums(hidden, weights, pair)
    back, core, hidden = barrier((back, core, hidden))
    back = [swap(sums, "tgt", 1) for sums in back]
    (own,) = partial_sums(hidden, weights, (0,), (tokens, swap(core, "src", 1)), jnp.float32)
    return own, *back


def on_device(tokens, sentence_ids, inner_weight, outer_weight, grid_rows, candidates, targets):
    features = tokens.shape[1]
    src_count = lax.axis_size("src")
    tgt_count = lax.axis_size("tgt")
    src_index = lax.axis_index("src")
    tgt_index = lax.axis_index("tgt")
    per_block = SENT_DEV // src_count
    block_rows = tgt_count * SENT_DEV

    column_blocks = targets.shape[0] // TBLK
    target_units = listed_units(candidates, targets)

    summands = feed_forward(tokens, inner_weight, outer_weight)
    order_key = (grid_rows // block_rows ^ src_index) * per_block + grid_rows % per_block
    held = local_call(
        pool_kernel,
        shape((SENT_DEV, features), jnp.bfloat16),
        (sentence_ids, order_key.reshape(1, -1), *summands),
        20 * tokens.shape[0] * features,
    )
    held = held.reshape(src_count, 1, per_block, features)
    for bit in reversed(bits_of("src", 1)):
        held = jnp.concatenate([held[:bit], swap(held[bit:], "src", bit)], axis=1)
    mine = held.reshape(SENT_DEV, features)
    parts = [mine] + [swap(mine, "tgt", offset) for offset in range(1, tgt_count)]
    origin = jnp.arange(1, dtype=jnp.int32)
    for bit in reversed(bits_of("src", 1)):
        origin = jnp.concatenate([origin, origin ^ bit])
    from_src = (origin ^ src_index)[None, :, None]
    from_tgt = (jnp.arange(tgt_count, dtype=jnp.int32) ^ tgt_index)[:, None, None]
    place = (from_src * tgt_count + from_tgt) * per_block + jnp.arange(per_block, dtype=jnp.int32)
    place = place.reshape(1, -1) ^ (tgt_index * SENT_DEV)

    pairs = MOST * TBLK
    expo, column_total, row_total = local_call(
        score_kernel,
        (
            shape((block_rows, pairs), jnp.float32),
            shape((column_blocks, TBLK), jnp.float32),
            shape((block_rows, 1), jnp.float32),
        ),
        (candidates, place, target_units, *parts),
        2 * block_rows * pairs * features,
        (*SLOTS, pltpu.VMEM((block_rows, features), jnp.bfloat16)),
        scalars=1,
    )
    for bit in bits_of("src", 1):
        column_total = column_total + swap(column_total, "src", bit)
    own, sent = local_call(
        match_kernel,
        (
            shape((SENT_DEV, features + LANES), jnp.float32),
            shape((block_rows - SENT_DEV, features + LANES), jnp.bfloat16),
        ),
        (candidates, expo, column_total, row_total, target_units),
        2 * block_rows * pairs * features,
        SLOTS,
        scalars=1,
    )
    received = [
        swap(sent[(offset - 1) * SENT_DEV : offset * SENT_DEV], "tgt", offset)
        for offset in range(1, tgt_count)
    ]
    matched, log_mass = local_call(
        finish_kernel,
        (shape((SENT_DEV, features), jnp.bfloat16), shape((1, SENT_DEV), jnp.float32)),
        (own, *received),
        8 * SENT_DEV * features,
    )
    return (matched, log_mass.reshape(SENT_DEV))


def solution(mesh):
    in_specs = (
        P(("groups", "src", "tgt"), None),
        P(("groups", "src", "tgt"), None),
        P(("src", "tgt"), None),
        P(("src", "tgt"), None),
        P(("groups", "src", "tgt")),
        P(("groups", "src"), None),
        P(("groups", "tgt"), None),
    )
    out_specs = (P(("groups", "src", "tgt"), None), P(("groups", "src", "tgt")))
    return jax.shard_map(
        on_device, mesh=mesh, in_specs=in_specs, out_specs=out_specs, check_vma=False
    )
```

```python
import functools
import math

import jax
import jax.numpy as jnp
from jax import lax
from jax.experimental import pallas as pl
from jax.experimental.pallas import tpu as pltpu
from jax.sharding import PartitionSpec as P

SENT_DEV = 32
TBLK = 256
MOST = 4
LANES = 128


SCORE_SCALE = 32.0


def bits_of(axis, first):
    size, bit, bits = lax.axis_size(axis), first, []
    while bit < size:
        bits.append(bit)
        bit *= 2
    return bits


def swap(values, axis, offset):
    return lax.ppermute(values, axis, [(i, i ^ offset) for i in range(lax.axis_size(axis))])


def local_call(
    kernel, out_shape, args, flops, scratch=(), scalars=0, near=0, place=pltpu.VMEM, vmem=16
):
    outs = out_shape if isinstance(out_shape, tuple) else (out_shape,)
    moved = sum(math.prod(a.shape) * a.dtype.itemsize for a in (*args, *outs))
    return pl.pallas_call(
        kernel,
        out_shape=out_shape,
        in_specs=[pl.BlockSpec(memory_space=pltpu.SMEM)] * scalars
        + [pl.BlockSpec(memory_space=pltpu.VMEM)] * near
        + [pl.BlockSpec(memory_space=place)] * (len(args) - scalars - near),
        out_specs=jax.tree.map(lambda _: pl.BlockSpec(memory_space=pltpu.VMEM), out_shape),
        scratch_shapes=scratch,
        compiler_params=pltpu.CompilerParams(vmem_limit_bytes=vmem * 2**20),
        cost_estimate=pl.CostEstimate(flops=flops, bytes_accessed=moved, transcendentals=0),
    )(*args)


def shape(dims, dtype):
    return jax.ShapeDtypeStruct(tuple(dims), dtype)


def unit_of(floats):
    square = jnp.mean(floats * floats, axis=-1, keepdims=True)
    return (floats * lax.rsqrt(square + 1e-06) * (1.0 / math.sqrt(floats.shape[-1]))).astype(
        jnp.bfloat16
    )


def dot(left, right, contract, **more):
    return lax.dot_general(
        left, right, ((contract[:1], contract[1:]), ((), ())),
        preferred_element_type=jnp.float32, **more
    )


def gather_refs(refs, held):
    start = 0
    for ref in refs:
        held[start : start + ref.shape[0], :] = ref[...]
        start += ref.shape[0]


def fetches(refs, held, sems, paired=None):
    start, copies = 0, []
    for index, ref in enumerate(refs):
        count = ref.shape[0]
        place = start
        if paired is not None and index in (paired, paired + 1):
            first = lax.axis_index("groups")
            step = first if index == paired else -first
            place = pl.multiple_of(start + step * count, count)
        copies.append(
            pltpu.make_async_copy(ref, held.at[pl.ds(place, count)], sems.at[index])
        )
        start += count
    for copy in copies:
        copy.start()
    return copies


def slice_kernel(inner, outer, inner_half, outer_half, sems):
    half = inner_half.shape[0]
    rows = pl.ds(pl.multiple_of(lax.axis_index("groups") * half, half), half)
    copies = [
        pltpu.make_async_copy(inner.at[rows], inner_half, sems.at[0]),
        pltpu.make_async_copy(outer.at[rows], outer_half, sems.at[1]),
    ]
    for copy in copies:
        copy.start()
    for copy in copies:
        copy.wait()


def weight_halves(inner, outer):
    units, features = inner.shape
    return local_call(
        slice_kernel,
        (shape((units // 2, features), jnp.bfloat16),) * 2,
        (inner, outer),
        0,
        (pltpu.SemaphoreType.DMA((2,)),),
        place=pl.ANY,
        vmem=58,
    )


def hidden_kernel(count, *refs):
    tokens, weights, (out, held, sems) = refs[:count], refs[count:-3], refs[-3:]
    for copy in fetches(weights, held, sems):
        copy.wait()
    start = 0
    for token in tokens:
        part = pl.ds(start, token.shape[0])
        product = dot(token[...], held[...], (1, 1))
        out[part, :] = (
            product * 0.5 * (1.0 + lax.erf(product * math.sqrt(0.5)))
        ).astype(jnp.bfloat16)
        start += token.shape[0]


def hidden_units(tokens, weights):
    features = weights[0].shape[1]
    rows = sum(t.shape[0] for t in tokens)
    units = sum(w.shape[0] for w in weights)
    return local_call(
        functools.partial(hidden_kernel, len(tokens)),
        shape((rows, units), jnp.bfloat16),
        (*tokens, *weights),
        2 * rows * units * features,
        (
            pltpu.VMEM((units, features), jnp.bfloat16),
            pltpu.SemaphoreType.DMA((len(weights),)),
        ),
        near=len(tokens),
        place=pl.ANY,
    )


def partial_kernel(blocks, added, near, far, *refs):
    terms, refs = refs[:added], refs[added:]
    split = near.shape[1]
    weights, outs, (held, sems) = refs[: -len(blocks) - 2], refs[-len(blocks) - 2 : -2], refs[-2:]
    for copy in fetches(weights, held, sems, paired=1):
        copy.wait()
    for index, out in zip(blocks, outs):
        rows = out.shape[0]
        part = pl.ds(index * rows, rows)
        sums = dot(near[part, :], held[:split, :], (1, 0)) + dot(far[part, :], held[split:, :], (1, 0))
        for term in terms:
            sums = sums + term[...].astype(jnp.float32)
        out[...] = sums.astype(out.dtype)


def return_kernel(near, far, core, *refs):
    weights, (first, second, held, sems) = refs[:-4], refs[-4:]
    for copy in fetches(weights, held, sems, paired=1):
        copy.wait()
    rows, split = first.shape[0], near.shape[1]
    for index, out in enumerate((first, second)):
        part = pl.ds((2 + index) * rows, rows)
        sums = dot(near[part, :], held[:split, :], (1, 0)) + dot(far[part, :], held[split:, :], (1, 0))
        out[...] = (sums + core[index * rows : (index + 1) * rows, :].astype(jnp.float32)).astype(
            out.dtype
        )


def return_sums(hidden, weights, core):
    rows, features = core.shape
    units = hidden[0].shape[1] + hidden[1].shape[1]
    return local_call(
        return_kernel,
        (shape((rows // 2, features), jnp.bfloat16),) * 2,
        (*hidden, core, *weights),
        2 * rows * units * features,
        (
            pltpu.VMEM((units, features), jnp.bfloat16),
            pltpu.SemaphoreType.DMA((len(weights),)),
        ),
        near=3,
        place=pl.ANY,
    )


def partial_sums(hidden, weights, blocks, terms=(), dtype=jnp.bfloat16):
    rows, features = hidden[0].shape[0] // 4, weights[0].shape[1]
    units = hidden[0].shape[1] + hidden[1].shape[1]
    return local_call(
        functools.partial(partial_kernel, blocks, len(terms)),
        (shape((rows, features), dtype),) * len(blocks),
        (*hidden, *terms, *weights),
        2 * len(blocks) * rows * units * features,
        (
            pltpu.VMEM((units, features), jnp.bfloat16),
            pltpu.SemaphoreType.DMA((len(weights),)),
        ),
        near=2 + len(terms),
        place=pl.ANY,
    )


def pool_kernel(identity, order, own, first, second, out):
    summed = own[...] + jnp.concatenate([first[...], second[...]], axis=0).astype(jnp.float32)
    center = jnp.mean(summed, axis=-1, keepdims=True)
    moved = summed - center
    spread = jnp.mean(moved * moved, axis=-1, keepdims=True)
    normed = moved * lax.rsqrt(spread + 1e-05)
    sentences = out.shape[0]
    members = (
        identity[...] == lax.broadcasted_iota(jnp.int32, (sentences, own.shape[0]), 0)
    ).astype(jnp.float32)
    sums = dot(members, normed, (1, 0), precision=lax.Precision.HIGHEST)
    unit = unit_of(sums / jnp.sum(members, axis=1, keepdims=True))
    sort = (order[...] == lax.broadcasted_iota(jnp.int32, (sentences, sentences), 0)).astype(
        jnp.bfloat16
    )
    out[...] = dot(sort, unit, (1, 0)).astype(jnp.bfloat16)


def find_slots(listed, slots, valid, blocks):
    column = lax.axis_index("tgt")
    for slot in range(MOST):
        slots[slot] = 0
        valid[slot] = 0
    count = jnp.int32(0)
    for index in range(listed.shape[1]):
        block = listed[0, index]
        here = lax.div(block, blocks) == column

        @pl.when(here)
        def _():
            slots[count] = lax.rem(block, blocks)
            valid[count] = 1

        count = count + here.astype(jnp.int32)


SLOTS = (pltpu.SMEM((MOST,), jnp.int32),) * 2


def target_kernel(listed, targets, out, slots, valid, tiles, sems):
    find_slots(listed, slots, valid, targets.shape[0] // TBLK)
    copies = [
        pltpu.make_async_copy(
            targets.at[pl.ds(pl.multiple_of(slots[slot] * TBLK, TBLK), TBLK)],
            tiles.at[slot],
            sems.at[slot],
        )
        for slot in range(MOST)
    ]
    for copy in copies:
        copy.start()
    for slot, copy in enumerate(copies):
        copy.wait()
        out[slot * TBLK : (slot + 1) * TBLK, :] = unit_of(tiles[slot].astype(jnp.float32))


def listed_units(candidates, targets):
    features = targets.shape[1]
    return local_call(
        target_kernel,
        shape((MOST * TBLK, features), jnp.bfloat16),
        (candidates, targets),
        8 * MOST * TBLK * features,
        (
            *SLOTS,
            pltpu.VMEM((MOST, TBLK, features), jnp.bfloat16),
            pltpu.SemaphoreType.DMA((MOST,)),
        ),
        scalars=1,
        place=pl.ANY,
    )


def score_kernel(listed, place, units, *refs):
    parts, (expo, columns, row_total, slots, valid, held) = refs[:-6], refs[-6:]
    find_slots(listed, slots, valid, columns.shape[0])
    gather_refs(parts, held)
    rows = expo.shape[0]
    sort = (place[...] == lax.broadcasted_iota(jnp.int32, (rows, rows), 0)).astype(jnp.bfloat16)
    block = dot(sort, held[...], (1, 0)).astype(jnp.bfloat16)
    scores = dot(block, units[...], (1, 1))
    columns[...] = jnp.zeros_like(columns)
    total = jnp.zeros((rows, 1), jnp.float32)
    for slot in range(MOST):
        part = slice(slot * TBLK, (slot + 1) * TBLK)
        values = jnp.exp(SCORE_SCALE * scores[:, part]) * valid[slot].astype(jnp.float32)
        expo[:, part] = values
        total = total + jnp.sum(values, axis=1, keepdims=True)
        column = jnp.sum(values, axis=0, keepdims=True)

        @pl.when(valid[slot] > 0)
        def _():
            columns[pl.ds(slots[slot], 1), :] = column

    row_total[...] = total


def extra_columns(values):
    lane = lax.broadcasted_iota(jnp.int32, (values[0].shape[0], LANES), 1)
    out = jnp.zeros(lane.shape, jnp.float32)
    for index, value in enumerate(values):
        out = jnp.where(lane == index, value, out)
    return out


def thirds(value):
    first = value.astype(jnp.bfloat16).astype(jnp.float32)
    second = (value - first).astype(jnp.bfloat16).astype(jnp.float32)
    return [first, second, value - first - second]


def match_kernel(listed, expo, columns, row_total, units, own, sent, slots, valid):
    find_slots(listed, slots, valid, columns.shape[0])
    rows = own.shape[0]
    features = units.shape[1]
    mass = jnp.zeros((expo.shape[0], 1), jnp.float32)
    weights = []
    for slot in range(MOST):
        part = pl.ds(slot * TBLK, TBLK)
        values = expo[:, part]
        listed = valid[slot].astype(jnp.float32)
        divisor = jnp.where(listed > 0, columns[pl.ds(slots[slot], 1), :], 1.0)
        mutual = values * (values / divisor)
        mass = mass + jnp.sum(mutual, axis=1, keepdims=True)
        weights.append(mutual.astype(jnp.bfloat16))
    numer = dot(jnp.concatenate(weights, axis=1), units[...], (1, 0))
    totals = row_total[...]
    zero = jnp.zeros((rows, 1), jnp.float32)
    own[:, :features] = numer[:rows]
    own[:, features:] = extra_columns([mass[:rows], zero, zero, totals[:rows]])
    sent[:, :features] = numer[rows:].astype(jnp.bfloat16)
    sent[:, features:] = extra_columns(thirds(mass[rows:]) + thirds(totals[rows:])).astype(
        jnp.bfloat16
    )


def finish_kernel(own, *refs):
    parts, (matched, log_mass) = refs[:-2], refs[-2:]
    rows, features = matched.shape
    total = own[...]
    for part in parts:
        total = total + part[...].astype(jnp.float32)
    numer = total[:, :features]
    square = jnp.mean(numer * numer, axis=-1, keepdims=True)
    matched[...] = (numer * lax.rsqrt(square + 1e-06)).astype(jnp.bfloat16)
    extra = total[:, features:]
    lane = lax.broadcasted_iota(jnp.int32, extra.shape, 1)
    mass = jnp.sum(jnp.where(lane < 3, extra, 0.0), axis=1, keepdims=True)
    whole = jnp.sum(jnp.where(lane < 3, 0.0, extra), axis=1, keepdims=True)
    ratio = mass / whole
    same = lax.broadcasted_iota(jnp.int32, (rows, rows), 0) == lax.broadcasted_iota(
        jnp.int32, (rows, rows), 1
    )
    log_mass[...] = jnp.log(jnp.sum(jnp.where(same, ratio, 0.0), axis=0, keepdims=True))


def far_piece(half):
    held = half
    for axis, bit in [("tgt", b) for b in bits_of("tgt", 2)] + [("src", b) for b in bits_of("src", 4)]:
        held = jnp.concatenate([held, swap(held, axis, bit)])
    return held[half.shape[0] :]


def feed_forward(tokens, inner_weight, outer_weight):
    barrier = lax.optimization_barrier
    inner_half, outer_half = weight_halves(inner_weight, outer_weight)
    inner_x, outer_x = swap(inner_weight, "src", 2), swap(outer_half, "src", 2)
    inner_far, outer_far = far_piece(inner_half), far_piece(outer_half)
    neighbour = swap(barrier((tokens, inner_half))[0], "tgt", 1)
    inner_far_x = swap(inner_far, "src", 2)

    outer_y = swap(outer_x, "groups", 1)
    inner_far, outer_far, inner_far_x, outer_y, inner_x = barrier(
        (inner_far, outer_far, inner_far_x, outer_y, inner_x)
    )
    inner_far_y = swap(inner_far, "groups", 1)
    outer_far_x, outer_far_y = swap(outer_far, "src", 2), swap(outer_far, "groups", 1)
    inner_square = [inner_far_x, inner_far_y, swap(inner_far_y, "src", 2)]
    outer_square = [outer_far_x, outer_far_y, swap(outer_far_x, "groups", 1)]
    shared = [tokens, neighbour, swap(tokens, "src", 1), swap(neighbour, "src", 1)]
    inner_square[2], outer_square[1] = barrier((inner_square[2], outer_square[1]))
    hidden = [
        hidden_units(shared, [inner_weight, inner_x, inner_far, inner_square[0]]),
        hidden_units(shared, inner_square[1:]),
    ]

    weights = [outer_weight, outer_x, outer_y, outer_far, *outer_square]
    (pair,) = partial_sums(hidden, weights, (3,))
    hidden, pair = barrier((hidden, pair))
    (core,) = partial_sums(hidden, weights, (2,))
    pair, core = barrier((swap(pair, "src", 1), core))
    back = return_sums(hidden, weights, pair)
    back, core, hidden = barrier((back, core, hidden))
    back = [swap(sums, "tgt", 1) for sums in back]
    (own,) = partial_sums(hidden, weights, (0,), (tokens, swap(core, "src", 1)), jnp.float32)
    return own, *back


def on_device(tokens, sentence_ids, inner_weight, outer_weight, grid_rows, candidates, targets):
    features = tokens.shape[1]
    src_count = lax.axis_size("src")
    tgt_count = lax.axis_size("tgt")
    src_index = lax.axis_index("src")
    tgt_index = lax.axis_index("tgt")
    per_block = SENT_DEV // src_count
    block_rows = tgt_count * SENT_DEV

    column_blocks = targets.shape[0] // TBLK
    target_units = listed_units(candidates, targets)

    summands = feed_forward(tokens, inner_weight, outer_weight)
    order_key = (grid_rows // block_rows ^ src_index) * per_block + grid_rows % per_block
    held = local_call(
        pool_kernel,
        shape((SENT_DEV, features), jnp.bfloat16),
        (sentence_ids, order_key.reshape(1, -1), *summands),
        20 * tokens.shape[0] * features,
    )
    held = held.reshape(src_count, per_block, features)
    mine = jnp.concatenate(
        [held[0]] + [swap(held[offset], "src", offset) for offset in range(1, src_count)]
    )
    parts = [mine] + [swap(mine, "tgt", offset) for offset in range(1, tgt_count)]
    origin = jnp.arange(src_count, dtype=jnp.int32)
    from_src = (origin ^ src_index)[None, :, None]
    from_tgt = (jnp.arange(tgt_count, dtype=jnp.int32) ^ tgt_index)[:, None, None]
    place = (from_src * tgt_count + from_tgt) * per_block + jnp.arange(per_block, dtype=jnp.int32)
    place = place.reshape(1, -1) ^ (tgt_index * SENT_DEV)

    pairs = MOST * TBLK
    expo, column_total, row_total = local_call(
        score_kernel,
        (
            shape((block_rows, pairs), jnp.float32),
            shape((column_blocks, TBLK), jnp.float32),
            shape((block_rows, 1), jnp.float32),
        ),
        (candidates, place, target_units, *parts),
        2 * block_rows * pairs * features,
        (*SLOTS, pltpu.VMEM((block_rows, features), jnp.bfloat16)),
        scalars=1,
    )
    for bit in bits_of("src", 1):
        column_total = column_total + swap(column_total, "src", bit)
    own, sent = local_call(
        match_kernel,
        (
            shape((SENT_DEV, features + LANES), jnp.float32),
            shape((block_rows - SENT_DEV, features + LANES), jnp.bfloat16),
        ),
        (candidates, expo, column_total, row_total, target_units),
        2 * block_rows * pairs * features,
        SLOTS,
        scalars=1,
    )
    received = [
        swap(sent[(offset - 1) * SENT_DEV : offset * SENT_DEV], "tgt", offset)
        for offset in range(1, tgt_count)
    ]
    matched, log_mass = local_call(
        finish_kernel,
        (shape((SENT_DEV, features), jnp.bfloat16), shape((1, SENT_DEV), jnp.float32)),
        (own, *received),
        8 * SENT_DEV * features,
    )
    return (matched, log_mass.reshape(SENT_DEV))


def solution(mesh):
    in_specs = (
        P(("groups", "src", "tgt"), None),
        P(("groups", "src", "tgt"), None),
        P(("src", "tgt"), None),
        P(("src", "tgt"), None),
        P(("groups", "src", "tgt")),
        P(("groups", "src"), None),
        P(("groups", "tgt"), None),
    )
    out_specs = (P(("groups", "src", "tgt"), None), P(("groups", "src", "tgt")))
    return jax.shard_map(
        on_device, mesh=mesh, in_specs=in_specs, out_specs=out_specs, check_vma=False
    )
```

```python
import functools
import math

import jax
import jax.numpy as jnp
from jax import lax
from jax.experimental import pallas as pl
from jax.experimental.pallas import tpu as pltpu
from jax.sharding import PartitionSpec as P

SENT_DEV = 32
TBLK = 256
MOST = 4
LANES = 128


SCORE_SCALE = 32.0


def bits_of(axis, first):
    size, bit, bits = lax.axis_size(axis), first, []
    while bit < size:
        bits.append(bit)
        bit *= 2
    return bits


def swap(values, axis, offset):
    return lax.ppermute(values, axis, [(i, i ^ offset) for i in range(lax.axis_size(axis))])


def local_call(
    kernel, out_shape, args, flops, scratch=(), scalars=0, near=0, place=pltpu.VMEM, vmem=16
):
    outs = out_shape if isinstance(out_shape, tuple) else (out_shape,)
    moved = sum(math.prod(a.shape) * a.dtype.itemsize for a in (*args, *outs))
    return pl.pallas_call(
        kernel,
        out_shape=out_shape,
        in_specs=[pl.BlockSpec(memory_space=pltpu.SMEM)] * scalars
        + [pl.BlockSpec(memory_space=pltpu.VMEM)] * near
        + [pl.BlockSpec(memory_space=place)] * (len(args) - scalars - near),
        out_specs=jax.tree.map(lambda _: pl.BlockSpec(memory_space=pltpu.VMEM), out_shape),
        scratch_shapes=scratch,
        compiler_params=pltpu.CompilerParams(vmem_limit_bytes=vmem * 2**20),
        cost_estimate=pl.CostEstimate(flops=flops, bytes_accessed=moved, transcendentals=0),
    )(*args)


def shape(dims, dtype):
    return jax.ShapeDtypeStruct(tuple(dims), dtype)


def unit_of(floats):
    square = jnp.mean(floats * floats, axis=-1, keepdims=True)
    return (floats * lax.rsqrt(square + 1e-06) * (1.0 / math.sqrt(floats.shape[-1]))).astype(
        jnp.bfloat16
    )


def dot(left, right, contract, **more):
    return lax.dot_general(
        left, right, ((contract[:1], contract[1:]), ((), ())),
        preferred_element_type=jnp.float32, **more
    )


def gather_refs(refs, held):
    start = 0
    for ref in refs:
        held[start : start + ref.shape[0], :] = ref[...]
        start += ref.shape[0]


def fetches(refs, held, sems, paired=None):
    start, copies = 0, []
    for index, ref in enumerate(refs):
        count = ref.shape[0]
        place = start
        if paired is not None and index in (paired, paired + 1):
            first = lax.axis_index("groups")
            step = first if index == paired else -first
            place = pl.multiple_of(start + step * count, count)
        copies.append(
            pltpu.make_async_copy(ref, held.at[pl.ds(place, count)], sems.at[index])
        )
        start += count
    for copy in copies:
        copy.start()
    return copies


def slice_kernel(inner, outer, inner_half, outer_half, sems):
    half = inner_half.shape[0]
    rows = pl.ds(pl.multiple_of(lax.axis_index("groups") * half, half), half)
    copies = [
        pltpu.make_async_copy(inner.at[rows], inner_half, sems.at[0]),
        pltpu.make_async_copy(outer.at[rows], outer_half, sems.at[1]),
    ]
    for copy in copies:
        copy.start()
    for copy in copies:
        copy.wait()


def weight_halves(inner, outer):
    units, features = inner.shape
    return local_call(
        slice_kernel,
        (shape((units // 2, features), jnp.bfloat16),) * 2,
        (inner, outer),
        0,
        (pltpu.SemaphoreType.DMA((2,)),),
        place=pl.ANY,
        vmem=58,
    )


def hidden_kernel(count, *refs):
    tokens, weights, (out, held, sems) = refs[:count], refs[count:-3], refs[-3:]
    for copy in fetches(weights, held, sems):
        copy.wait()
    start = 0
    for token in tokens:
        part = pl.ds(start, token.shape[0])
        product = dot(token[...], held[...], (1, 1))
        out[part, :] = (
            product * 0.5 * (1.0 + lax.erf(product * math.sqrt(0.5)))
        ).astype(jnp.bfloat16)
        start += token.shape[0]


def hidden_units(tokens, weights):
    features = weights[0].shape[1]
    rows = sum(t.shape[0] for t in tokens)
    units = sum(w.shape[0] for w in weights)
    return local_call(
        functools.partial(hidden_kernel, len(tokens)),
        shape((rows, units), jnp.bfloat16),
        (*tokens, *weights),
        2 * rows * units * features,
        (
            pltpu.VMEM((units, features), jnp.bfloat16),
            pltpu.SemaphoreType.DMA((len(weights),)),
        ),
        near=len(tokens),
        place=pl.ANY,
    )


def partial_kernel(blocks, added, near, far, *refs):
    terms, refs = refs[:added], refs[added:]
    split = near.shape[1]
    weights, outs, (held, sems) = refs[: -len(blocks) - 2], refs[-len(blocks) - 2 : -2], refs[-2:]
    for copy in fetches(weights, held, sems, paired=1):
        copy.wait()
    for index, out in zip(blocks, outs):
        rows = out.shape[0]
        part = pl.ds(index * rows, rows)
        sums = dot(near[part, :], held[:split, :], (1, 0)) + dot(far[part, :], held[split:, :], (1, 0))
        for term in terms:
            sums = sums + term[...].astype(jnp.float32)
        out[...] = sums.astype(out.dtype)


def return_kernel(near, far, core, *refs):
    weights, (first, second, held, sems) = refs[:-4], refs[-4:]
    for copy in fetches(weights, held, sems, paired=1):
        copy.wait()
    rows, split = first.shape[0], near.shape[1]
    for index, out in enumerate((first, second)):
        part = pl.ds((2 + index) * rows, rows)
        sums = dot(near[part, :], held[:split, :], (1, 0)) + dot(far[part, :], held[split:, :], (1, 0))
        out[...] = (sums + core[index * rows : (index + 1) * rows, :].astype(jnp.float32)).astype(
            out.dtype
        )


def return_sums(hidden, weights, core):
    rows, features = core.shape
    units = hidden[0].shape[1] + hidden[1].shape[1]
    return local_call(
        return_kernel,
        (shape((rows // 2, features), jnp.bfloat16),) * 2,
        (*hidden, core, *weights),
        2 * rows * units * features,
        (
            pltpu.VMEM((units, features), jnp.bfloat16),
            pltpu.SemaphoreType.DMA((len(weights),)),
        ),
        near=3,
        place=pl.ANY,
    )


def partial_sums(hidden, weights, blocks, terms=(), dtype=jnp.bfloat16):
    rows, features = hidden[0].shape[0] // 4, weights[0].shape[1]
    units = hidden[0].shape[1] + hidden[1].shape[1]
    return local_call(
        functools.partial(partial_kernel, blocks, len(terms)),
        (shape((rows, features), dtype),) * len(blocks),
        (*hidden, *terms, *weights),
        2 * len(blocks) * rows * units * features,
        (
            pltpu.VMEM((units, features), jnp.bfloat16),
            pltpu.SemaphoreType.DMA((len(weights),)),
        ),
        near=2 + len(terms),
        place=pl.ANY,
    )


def pool_kernel(identity, order, own, first, second, out):
    summed = own[...] + jnp.concatenate([first[...], second[...]], axis=0).astype(jnp.float32)
    center = jnp.mean(summed, axis=-1, keepdims=True)
    moved = summed - center
    spread = jnp.mean(moved * moved, axis=-1, keepdims=True)
    normed = moved * lax.rsqrt(spread + 1e-05)
    sentences = out.shape[0]
    members = (
        identity[...] == lax.broadcasted_iota(jnp.int32, (sentences, own.shape[0]), 0)
    ).astype(jnp.float32)
    sums = dot(members, normed, (1, 0), precision=lax.Precision.HIGHEST)
    unit = unit_of(sums / jnp.sum(members, axis=1, keepdims=True))
    sort = (order[...] == lax.broadcasted_iota(jnp.int32, (sentences, sentences), 0)).astype(
        jnp.bfloat16
    )
    out[...] = dot(sort, unit, (1, 0)).astype(jnp.bfloat16)


def find_slots(listed, slots, valid, blocks):
    column = lax.axis_index("tgt")
    for slot in range(MOST):
        slots[slot] = 0
        valid[slot] = 0
    count = jnp.int32(0)
    for index in range(listed.shape[1]):
        block = listed[0, index]
        here = lax.div(block, blocks) == column

        @pl.when(here)
        def _():
            slots[count] = lax.rem(block, blocks)
            valid[count] = 1

        count = count + here.astype(jnp.int32)


SLOTS = (pltpu.SMEM((MOST,), jnp.int32),) * 2


def target_kernel(listed, targets, out, slots, valid, tiles, sems):
    find_slots(listed, slots, valid, targets.shape[0] // TBLK)
    copies = [
        pltpu.make_async_copy(
            targets.at[pl.ds(pl.multiple_of(slots[slot] * TBLK, TBLK), TBLK)],
            tiles.at[slot],
            sems.at[slot],
        )
        for slot in range(MOST)
    ]
    for copy in copies:
        copy.start()
    for slot, copy in enumerate(copies):
        copy.wait()
        out[slot * TBLK : (slot + 1) * TBLK, :] = unit_of(tiles[slot].astype(jnp.float32))


def listed_units(candidates, targets):
    features = targets.shape[1]
    return local_call(
        target_kernel,
        shape((MOST * TBLK, features), jnp.bfloat16),
        (candidates, targets),
        8 * MOST * TBLK * features,
        (
            *SLOTS,
            pltpu.VMEM((MOST, TBLK, features), jnp.bfloat16),
            pltpu.SemaphoreType.DMA((MOST,)),
        ),
        scalars=1,
        place=pl.ANY,
    )


def score_kernel(listed, place, units, *refs):
    parts, (expo, columns, row_total, slots, valid, held) = refs[:-6], refs[-6:]
    find_slots(listed, slots, valid, columns.shape[0])
    gather_refs(parts, held)
    rows = expo.shape[0]
    sort = (place[...] == lax.broadcasted_iota(jnp.int32, (rows, rows), 0)).astype(jnp.bfloat16)
    block = dot(sort, held[...], (1, 0)).astype(jnp.bfloat16)
    scores = dot(block, units[...], (1, 1))
    columns[...] = jnp.zeros_like(columns)
    total = jnp.zeros((rows, 1), jnp.float32)
    for slot in range(MOST):
        part = slice(slot * TBLK, (slot + 1) * TBLK)
        values = jnp.exp(SCORE_SCALE * scores[:, part]) * valid[slot].astype(jnp.float32)
        expo[:, part] = values
        total = total + jnp.sum(values, axis=1, keepdims=True)
        column = jnp.sum(values, axis=0, keepdims=True)

        @pl.when(valid[slot] > 0)
        def _():
            columns[pl.ds(slots[slot], 1), :] = column

    row_total[...] = total


def extra_columns(values):
    lane = lax.broadcasted_iota(jnp.int32, (values[0].shape[0], LANES), 1)
    out = jnp.zeros(lane.shape, jnp.float32)
    for index, value in enumerate(values):
        out = jnp.where(lane == index, value, out)
    return out


def thirds(value):
    first = value.astype(jnp.bfloat16).astype(jnp.float32)
    second = (value - first).astype(jnp.bfloat16).astype(jnp.float32)
    return [first, second, value - first - second]


def match_kernel(listed, expo, columns, row_total, units, own, sent, slots, valid):
    find_slots(listed, slots, valid, columns.shape[0])
    rows = own.shape[0]
    features = units.shape[1]
    mass = jnp.zeros((expo.shape[0], 1), jnp.float32)
    weights = []
    for slot in range(MOST):
        part = pl.ds(slot * TBLK, TBLK)
        values = expo[:, part]
        listed = valid[slot].astype(jnp.float32)
        divisor = jnp.where(listed > 0, columns[pl.ds(slots[slot], 1), :], 1.0)
        mutual = values * (values / divisor)
        mass = mass + jnp.sum(mutual, axis=1, keepdims=True)
        weights.append(mutual.astype(jnp.bfloat16))
    numer = dot(jnp.concatenate(weights, axis=1), units[...], (1, 0))
    totals = row_total[...]
    zero = jnp.zeros((rows, 1), jnp.float32)
    own[:, :features] = numer[:rows]
    own[:, features:] = extra_columns([mass[:rows], zero, zero, totals[:rows]])
    sent[:, :features] = numer[rows:].astype(jnp.bfloat16)
    sent[:, features:] = extra_columns(thirds(mass[rows:]) + thirds(totals[rows:])).astype(
        jnp.bfloat16
    )


def finish_kernel(own, *refs):
    parts, (matched, log_mass) = refs[:-2], refs[-2:]
    rows, features = matched.shape
    total = own[...]
    for part in parts:
        total = total + part[...].astype(jnp.float32)
    numer = total[:, :features]
    square = jnp.mean(numer * numer, axis=-1, keepdims=True)
    matched[...] = (numer * lax.rsqrt(square + 1e-06)).astype(jnp.bfloat16)
    extra = total[:, features:]
    lane = lax.broadcasted_iota(jnp.int32, extra.shape, 1)
    mass = jnp.sum(jnp.where(lane < 3, extra, 0.0), axis=1, keepdims=True)
    whole = jnp.sum(jnp.where(lane < 3, 0.0, extra), axis=1, keepdims=True)
    ratio = mass / whole
    same = lax.broadcasted_iota(jnp.int32, (rows, rows), 0) == lax.broadcasted_iota(
        jnp.int32, (rows, rows), 1
    )
    log_mass[...] = jnp.log(jnp.sum(jnp.where(same, ratio, 0.0), axis=0, keepdims=True))


def far_piece(half):
    held = half
    for axis, bit in [("tgt", b) for b in bits_of("tgt", 2)] + [("src", b) for b in bits_of("src", 4)]:
        held = jnp.concatenate([held, swap(held, axis, bit)])
    return held[half.shape[0] :]


def feed_forward(tokens, inner_weight, outer_weight):
    barrier = lax.optimization_barrier
    inner_half, outer_half = weight_halves(inner_weight, outer_weight)
    inner_x, outer_x = swap(inner_weight, "src", 2), swap(outer_half, "src", 2)
    inner_far, outer_far = far_piece(inner_half), far_piece(outer_half)
    neighbour = swap(barrier((tokens, inner_half))[0], "tgt", 1)
    inner_far_x = swap(inner_far, "src", 2)

    outer_y = swap(outer_x, "groups", 1)
    inner_far, outer_far, inner_far_x, outer_y, inner_x = barrier(
        (inner_far, outer_far, inner_far_x, outer_y, inner_x)
    )
    inner_far_y = swap(inner_far, "groups", 1)
    outer_far_x, outer_far_y = swap(outer_far, "src", 2), swap(outer_far, "groups", 1)
    inner_square = [inner_far_x, inner_far_y, swap(inner_far_y, "src", 2)]
    outer_square = [outer_far_x, outer_far_y, swap(outer_far_x, "groups", 1)]
    shared = [tokens, neighbour, swap(tokens, "src", 1), swap(neighbour, "src", 1)]
    inner_square[2], outer_square[1] = barrier((inner_square[2], outer_square[1]))
    hidden = [
        hidden_units(shared, [inner_weight, inner_x, inner_far, inner_square[0]]),
        hidden_units(shared, inner_square[1:]),
    ]

    weights = [outer_weight, outer_x, outer_y, outer_far, *outer_square]
    (pair,) = partial_sums(hidden, weights, (3,))
    hidden, pair = barrier((hidden, pair))
    (core,) = partial_sums(hidden, weights, (2,))
    pair, core = barrier((swap(pair, "src", 1), core))
    back = return_sums(hidden, weights, pair)
    back, core, hidden = barrier((back, core, hidden))
    back = [swap(sums, "tgt", 1) for sums in back]
    (own,) = partial_sums(hidden, weights, (0,), (tokens, swap(core, "src", 1)), jnp.float32)
    return own, *back


def on_device(tokens, sentence_ids, inner_weight, outer_weight, grid_rows, candidates, targets):
    features = tokens.shape[1]
    src_count = lax.axis_size("src")
    tgt_count = lax.axis_size("tgt")
    src_index = lax.axis_index("src")
    tgt_index = lax.axis_index("tgt")
    per_block = SENT_DEV // src_count
    block_rows = tgt_count * SENT_DEV

    column_blocks = targets.shape[0] // TBLK
    target_units = listed_units(candidates, targets)

    summands = feed_forward(tokens, inner_weight, outer_weight)
    order_key = (grid_rows // block_rows ^ src_index) * per_block + grid_rows % per_block
    held = local_call(
        pool_kernel,
        shape((SENT_DEV, features), jnp.bfloat16),
        (sentence_ids, order_key.reshape(1, -1), *summands),
        20 * tokens.shape[0] * features,
    )
    held = held.reshape(src_count, per_block, features)
    mine = jnp.concatenate(
        [held[0]] + [swap(held[offset], "src", offset) for offset in range(1, src_count)]
    )
    parts = [swap(mine, "tgt", offset) for offset in reversed(range(1, tgt_count))]
    parts = [mine, *reversed(parts)]
    origin = jnp.arange(src_count, dtype=jnp.int32)
    from_src = (origin ^ src_index)[None, :, None]
    from_tgt = (jnp.arange(tgt_count, dtype=jnp.int32) ^ tgt_index)[:, None, None]
    place = (from_src * tgt_count + from_tgt) * per_block + jnp.arange(per_block, dtype=jnp.int32)
    place = place.reshape(1, -1) ^ (tgt_index * SENT_DEV)

    pairs = MOST * TBLK
    expo, column_total, row_total = local_call(
        score_kernel,
        (
            shape((block_rows, pairs), jnp.float32),
            shape((column_blocks, TBLK), jnp.float32),
            shape((block_rows, 1), jnp.float32),
        ),
        (candidates, place, target_units, *parts),
        2 * block_rows * pairs * features,
        (*SLOTS, pltpu.VMEM((block_rows, features), jnp.bfloat16)),
        scalars=1,
    )
    for bit in bits_of("src", 1):
        column_total = column_total + swap(column_total, "src", bit)
    own, sent = local_call(
        match_kernel,
        (
            shape((SENT_DEV, features + LANES), jnp.float32),
            shape((block_rows - SENT_DEV, features + LANES), jnp.bfloat16),
        ),
        (candidates, expo, column_total, row_total, target_units),
        2 * block_rows * pairs * features,
        SLOTS,
        scalars=1,
    )
    received = [
        swap(sent[(offset - 1) * SENT_DEV : offset * SENT_DEV], "tgt", offset)
        for offset in reversed(range(1, tgt_count))
    ]
    matched, log_mass = local_call(
        finish_kernel,
        (shape((SENT_DEV, features), jnp.bfloat16), shape((1, SENT_DEV), jnp.float32)),
        (own, *received),
        8 * SENT_DEV * features,
    )
    return (matched, log_mass.reshape(SENT_DEV))


def solution(mesh):
    in_specs = (
        P(("groups", "src", "tgt"), None),
        P(("groups", "src", "tgt"), None),
        P(("src", "tgt"), None),
        P(("src", "tgt"), None),
        P(("groups", "src", "tgt")),
        P(("groups", "src"), None),
        P(("groups", "tgt"), None),
    )
    out_specs = (P(("groups", "src", "tgt"), None), P(("groups", "src", "tgt")))
    return jax.shard_map(
        on_device, mesh=mesh, in_specs=in_specs, out_specs=out_specs, check_vma=False
    )
```
